512 devices in a mesh: gx: 32 (over z, x), gy: 16 (over y, core).
Axes of the slice: x: 4, y: 8, z: 8, core: 2. Of those that a mesh axis runs over, the one named last changes fastest.
Arguments:
- mentions: bfloat16 [131072, 768], P(('gx', 'gy')), may hold values from -64 to 64
- type_table: float32 [65536, 768], P(('gx', 'gy')), may hold values from -1.25 to 1.25
- adam_m: float32 [65536, 768], P(('gx', 'gy')), may hold values from -6 to 6
- adam_v: float32 [65536, 768], P(('gx', 'gy')), may hold values from 0.01 to 10
- logit_scale: float32 [1], replicated, may hold values from 3 to 6
- block_lists: int32 [1024, 16], P(('gx', 'gy')), may hold values from 0 to 511, as said below
- list_lengths: int32 [1024], P(('gx', 'gy')), may hold values from 4 to 16
- gold_slot: int32 [131072], P(('gx', 'gy')), may hold values from 0 to 15, as said below
- gold_row: int32 [131072], P(('gx', 'gy')), may hold values from 0 to 127
Outputs:
- new_table: float32 [65536, 768], P(('gx', 'gy'))
- new_first: float32 [65536, 768], P(('gx', 'gy'))
- new_second: float32 [65536, 768], P(('gx', 'gy'))
- mention_grad: bfloat16 [131072, 768], P(('gx', 'gy'))
- scale_grad: float32 [1], replicated
The draws below stay inside these ranges and needn't reach their ends.
Inputs may be any that keep to these rules, and one draw needn't show every extreme that they name: `block_lists`: row g names 16 distinct type blocks, all owned by devices with the same gy index as the device holding mention block g; only the first list_lengths[g] entries are used. `gold_slot`: below the list length of the mention's block.
All inputs are finite; a program needn't handle non-finite values.
Results may differ from the reference program's by a relative error of at most 0.0069.
Values may be sent and summed in bfloat16 or wider, within the bound.
No kernel may reach another device: no remote copies, remote signals or barrier semaphores. Data moves between devices by JAX's collectives and lax.ppermute only.
A program may use at most 128 MiB of HBM per device.

```python
import math
import jax
import jax.numpy as jnp
from jax import lax

D = 768
BLOCK = 128
KMIN = 4
KMAX = 16
MB_DEV = 2
TYPES = 65536
MBLOCKS = 1024
MENTIONS = 131072
N_GX = 32
N_GY = 16


def table_from(key):
    key = jax.random.fold_in(key, 101)
    normal_part = jnp.clip(jax.random.normal(key, (TYPES, D), jnp.float32), -6.0, 6.0)
    return normal_part / jnp.sqrt(jnp.float32(D))


def lists_from(key):
    key = jax.random.fold_in(key, 102)
    scores = jax.random.randint(key, (MBLOCKS, N_GX), 0, 1 << 20) * N_GX + jnp.arange(N_GX, dtype=jnp.int32)[None, :]
    order = jnp.argsort(scores, axis=1, stable=True)[:, :KMAX].astype(jnp.int32)
    device = jnp.arange(MBLOCKS, dtype=jnp.int32) // MB_DEV
    return (order * N_GY + (device % N_GY)[:, None]).astype(jnp.int32)


def lengths_from(key):
    key = jax.random.fold_in(key, 103)
    first_draw = jax.random.randint(key, (MBLOCKS,), 0, KMAX - KMIN + 1)
    second_draw = jax.random.randint(jax.random.fold_in(key, 1), (MBLOCKS,), 0, KMAX - KMIN + 1)
    lengths = KMIN + jnp.maximum(first_draw, second_draw)
    position = jax.random.randint(jax.random.fold_in(key, 2), (), 0, MBLOCKS)
    return jnp.where(jnp.arange(MBLOCKS, dtype=jnp.int32) == position, KMAX, lengths).astype(jnp.int32)


def slots_from(key):
    lengths = lengths_from(key)
    key = jax.random.fold_in(key, 104)
    return jax.random.randint(key, (MENTIONS,), 0, jnp.repeat(lengths, BLOCK)).astype(jnp.int32)


def gold_rows_from(key):
    key = jax.random.fold_in(key, 105)
    return jax.random.randint(key, (MENTIONS,), 0, BLOCK).astype(jnp.int32)


def device_factor(key, spread):
    key = jax.random.fold_in(key, 106)
    device = jnp.arange(MENTIONS, dtype=jnp.int32) // (MB_DEV * BLOCK)
    first_pos = (device // N_GY).astype(jnp.float32) / jnp.float32(max(N_GX - 1, 1))
    second_pos = (device % N_GY).astype(jnp.float32) / jnp.float32(max(N_GY - 1, 1))
    rising = 0.6 * jnp.exp(jnp.log(jnp.float32(3.0)) * 0.5 * (first_pos + second_pos))
    jitter = jnp.exp(jax.random.uniform(key, (N_GX * N_GY,), jnp.float32, -spread, spread))
    return rising * jitter[device]


def draw_mentions(key, part):
    own_key = jax.random.fold_in(key, 7)
    factors = device_factor(key, 0.29)
    values = factors[:, None] * jnp.clip(jax.random.normal(own_key, (MENTIONS, D), jnp.float32), -6.0, 6.0)
    return values.astype(jnp.bfloat16)


def draw_type_table(key, part):
    return table_from(key)


def draw_block_lists(key, part):
    return lists_from(key)


def draw_list_lengths(key, part):
    return lengths_from(key)


def draw_gold_slot(key, part):
    return slots_from(key)


def draw_gold_row(key, part):
    return gold_rows_from(key)


def level_of(stream_key, extent, pieces, smallest, high):
    factor_of, own = 1.0, jax.random.fold_in(stream_key, 6)
    for dim, parts in pieces:
        steps = jnp.exp(jax.random.uniform(jax.random.fold_in(own, dim), (parts,), jnp.float32, smallest / len(pieces), high / len(pieces)))
        factor_of = factor_of * jnp.repeat(steps, extent[dim] // parts).reshape([-1 if axis == dim else 1 for axis in range(len(extent))])
    return factor_of


def centred(key, extent, scale, reach, pieces=(), kind=jnp.bfloat16):
    entries = jax.random.normal(key, extent, jnp.float32) * scale
    if len(pieces) > 0:
        entries = level_of(key, extent, pieces, -0.22, 0.18) * entries
    return jnp.clip(entries, min=-reach, max=reach).astype(kind)


def setup_inputs(seed: int = 0) -> dict:
    streams_of = jax.random.split(jax.random.key(seed), 10)
    return {
        "mentions": draw_mentions(jax.random.fold_in(streams_of[9], 71), 0),
        "type_table": draw_type_table(jax.random.fold_in(streams_of[9], 71), 0),
        "adam_m": centred(streams_of[2], (TYPES, D), 1.0, 6.0, ((0, 512),), jnp.float32),
        "adam_v": jnp.clip(jnp.exp(math.log(10.0) - 6.9077553 * jax.random.uniform(streams_of[3], (TYPES, D), jnp.float32) ** level_of(streams_of[3], (TYPES, D), ((0, 512),), -0.2, 0.2)), 0.01, 10.0),
        "logit_scale": jnp.clip(jnp.exp(jax.random.uniform(streams_of[4], (1,), jnp.float32, math.log(3.0), math.log(6.0))), 3.0, 6.0),
        "block_lists": draw_block_lists(jax.random.fold_in(streams_of[9], 71), 0),
        "list_lengths": draw_list_lengths(jax.random.fold_in(streams_of[9], 71), 0),
        "gold_slot": draw_gold_slot(jax.random.fold_in(streams_of[9], 71), 0),
        "gold_row": draw_gold_row(jax.random.fold_in(streams_of[9], 71), 0),
    }


beta_one = 0.9
beta_two = 0.999
learn_rate = 0.02
adam_eps = 1e-08
first_fix = 0.9999734386011124
second_fix = 0.09520785288629038

def adam_rows(type_table, adam_m, adam_v, type_grad):
    moment_one = beta_one * adam_m + (1.0 - beta_one) * type_grad
    moment_two = beta_two * adam_v + (1.0 - beta_two) * type_grad * type_grad
    updated = type_table - learn_rate * (moment_one / first_fix) / (jnp.sqrt(moment_two / second_fix) + adam_eps)
    return (updated, moment_one, moment_two)

def reference(mentions, type_table, adam_m, adam_v, logit_scale, block_lists, list_lengths, gold_slot, gold_row):
    factor = logit_scale[0]
    device_count = N_GX * N_GY
    type_bf = type_table.astype(jnp.bfloat16).reshape(device_count, BLOCK, D)
    per_device = (mentions.reshape(device_count, MB_DEV, BLOCK, D), block_lists.reshape(device_count, MB_DEV, KMAX), list_lengths.reshape(device_count, MB_DEV), gold_slot.reshape(device_count, MB_DEV, BLOCK), gold_row.reshape(device_count, MB_DEV, BLOCK), jnp.arange(device_count, dtype=jnp.int32))

    def one_device(state_now, device_data):
        type_grad, scale_sum = state_now
        mention_rows, list_ids, list_len, slot_ids, gold_rows, device = device_data
        column = (device % N_GY).astype(jnp.int32)
        partial_value = jnp.zeros((N_GX, BLOCK, D), jnp.float32)
        grad_list = []
        for group in range(MB_DEV):
            candidates = jnp.take(type_bf, list_ids[group], axis=0).reshape(KMAX * BLOCK, D)
            raw_dot = jnp.dot(mention_rows[group], candidates.T, preferred_element_type=jnp.float32)
            scores = factor * raw_dot
            usable = jnp.repeat(jnp.arange(KMAX, dtype=jnp.int32) < list_len[group], BLOCK)[None, :]
            row_max = lax.optimization_barrier(jnp.max(jnp.where(usable, scores, -jnp.inf), axis=1, keepdims=True))
            row_total = lax.optimization_barrier(jnp.sum(jnp.where(usable, jnp.exp(scores - row_max), 0.0), axis=1, keepdims=True))
            log_total = row_max + jnp.log(row_total)
            weights = jnp.where(usable, jnp.exp(scores - log_total), 0.0)
            gold_column = slot_ids[group] * BLOCK + gold_rows[group]
            target = (jnp.arange(KMAX * BLOCK, dtype=jnp.int32)[None, :] == gold_column[:, None]).astype(jnp.float32)
            grad_scores = weights - target
            scale_sum = scale_sum + jnp.sum(grad_scores * raw_dot)
            grad_bf = grad_scores.astype(jnp.bfloat16)
            grad_list.append((factor * jnp.dot(grad_bf, candidates, preferred_element_type=jnp.float32)).astype(jnp.bfloat16))
            slot_grad = jnp.dot(grad_bf.T, mention_rows[group], preferred_element_type=jnp.float32).reshape(KMAX, BLOCK, D)
            owner_pick = ((list_ids[group] // N_GY)[:, None] == jnp.arange(N_GX, dtype=jnp.int32)[None, :]).astype(jnp.float32)
            partial_value = partial_value + jnp.einsum('kr,kbd->rbd', owner_pick, slot_grad, precision=lax.Precision.HIGHEST)
        rounded = lax.optimization_barrier((factor * partial_value).astype(jnp.bfloat16)).astype(jnp.float32)
        anchor = jnp.int32(0)
        current = lax.dynamic_slice(type_grad, (anchor, column, anchor, anchor), (N_GX, 1, BLOCK, D))
        type_grad = lax.dynamic_update_slice(type_grad, current + rounded[:, None], (anchor, column, anchor, anchor))
        return ((type_grad, scale_sum), jnp.stack(grad_list))
    start_state = (jnp.zeros((N_GX, N_GY, BLOCK, D), jnp.float32), jnp.float32(0.0))
    (type_grad, scale_sum), mention_grad = lax.scan(one_device, start_state, per_device)
    type_grad = type_grad.reshape(TYPES, D)
    new_table, new_first, new_second = adam_rows(type_table, adam_m, adam_v, type_grad)
    scale_grad = (scale_sum / MENTIONS).reshape(1)
    return (new_table, new_first, new_second, mention_grad.reshape(MENTIONS, D), scale_grad)
```

```python
import jax
import jax.numpy as jnp
from jax import lax
from jax.experimental import pallas as pl
from jax.experimental.pallas import tpu as pltpu
from jax.sharding import Mesh, PartitionSpec as P

beta_one = 0.9
beta_two = 0.999
learn_rate = 0.02
adam_eps = 1e-08
first_fix = 0.9999734386011124
second_fix = 0.09520785288629038

X_SIZE = 4
LOW = -1e30
META_ROWS = 16
STAT_ROWS = 8
f32 = jnp.float32
bf16 = jnp.bfloat16


def adam_rows(type_table, adam_m, adam_v, type_grad):
    moment_one = beta_one * adam_m + (1.0 - beta_one) * type_grad
    moment_two = beta_two * adam_v + (1.0 - beta_two) * type_grad * type_grad
    updated = type_table - learn_rate * (moment_one / first_fix) / (
        jnp.sqrt(moment_two / second_fix) + adam_eps
    )
    return (updated, moment_one, moment_two)


def scores_kernel(factor_ref, m_ref, t_ref, meta_ref, raw_ref, stat_ref):
    step = pl.program_id(0)
    factor = factor_ref[0]
    rows = m_ref.shape[1]
    chunks = t_ref.shape[0] // 128
    raw_ref[0] = lax.dot_general(
        t_ref[...], m_ref[0], (((1,), (1,)), ((), ())), preferred_element_type=f32
    )
    top = jnp.full((1, rows), LOW, f32)
    for c in range(chunks):
        live = meta_ref[0, c : c + 1, :] > 0.0
        part = jnp.max(factor * raw_ref[0, c * 128 : (c + 1) * 128, :], axis=0, keepdims=True)
        top = jnp.maximum(top, jnp.where(live, part, LOW))
    total = jnp.zeros((1, rows), f32)
    for c in range(chunks):
        live = meta_ref[0, c : c + 1, :] > 0.0
        scores = factor * raw_ref[0, c * 128 : (c + 1) * 128, :]
        part = jnp.sum(jnp.exp(scores - top), axis=0, keepdims=True)
        total = total + jnp.where(live, part, 0.0)
    stat = jnp.concatenate([top, total, jnp.zeros((STAT_ROWS - 2, rows), f32)], axis=0)
    for d in range(stat_ref.shape[0]):
        stat_ref[d, :, pl.ds(pl.multiple_of(step * rows, 128), rows)] = stat


def grads_kernel(factor_ref, raw_ref, meta_ref, stat_ref, m_ref, g_ref, type_ref, scale_ref, acc_ref, sum_ref):
    step = pl.program_id(0)
    factor = factor_ref[0]
    rows = m_ref.shape[1]
    chunks = raw_ref.shape[1] // 128
    tops = stat_ref[:, 0, :]
    sums = stat_ref[:, 1, :]
    top = jnp.max(tops, axis=0, keepdims=True)
    log_total = top + jnp.log(jnp.sum(sums * jnp.exp(tops - top), axis=0, keepdims=True))
    gold = meta_ref[0, chunks : chunks + 1, :].astype(jnp.int32)
    ids = lax.broadcasted_iota(jnp.int32, (128, rows), 0)
    scale = jnp.zeros((1, rows), f32)
    for c in range(chunks):
        live = meta_ref[0, c : c + 1, :] > 0.0
        raw = raw_ref[0, c * 128 : (c + 1) * 128, :]
        weights = jnp.where(live, jnp.exp(factor * raw - log_total), 0.0)
        grad = weights - jnp.where(ids + c * 128 == gold, 1.0, 0.0)
        scale = scale + jnp.sum(grad * raw, axis=0, keepdims=True)
        g_ref[0, c * 128 : (c + 1) * 128, :] = grad.astype(bf16)
    part = jnp.dot(g_ref[0], m_ref[0], preferred_element_type=f32)

    @pl.when(step == 0)
    def _():
        acc_ref[...] = part
        sum_ref[...] = scale

    @pl.when(step > 0)
    def _():
        acc_ref[...] += part
        sum_ref[...] += scale

    @pl.when(step == pl.num_programs(0) - 1)
    def _():
        type_ref[...] = (factor * acc_ref[...]).astype(bf16)
        scale_ref[...] = jnp.broadcast_to(jnp.sum(sum_ref[...], axis=1, keepdims=True), scale_ref.shape)


def mention_kernel(factor_ref, g_ref, t_ref, out_ref):
    part = lax.dot_general(
        g_ref[0], t_ref[...], (((0,), (0,)), ((), ())), preferred_element_type=f32
    )
    out_ref[0] = (factor_ref[0] * part).astype(bf16)


def params():
    return pltpu.CompilerParams(
        dimension_semantics=("arbitrary",), vmem_limit_bytes=40 * 1024 * 1024
    )


def per_device(
    mentions,
    type_table,
    adam_m,
    adam_v,
    logit_scale,
    block_lists,
    list_lengths,
    gold_slot,
    gold_row,
):
    z_size = lax.axis_size("gz")
    x_size = lax.axis_size("gx")
    col_count = lax.axis_size("gy")
    devices = z_size * x_size * col_count
    block_rows, width = type_table.shape
    groups, slot_max = block_lists.shape
    rows = groups * block_rows
    types = z_size * block_rows
    smem = pl.BlockSpec(memory_space=pltpu.SMEM)

    table = lax.all_gather(type_table.astype(bf16), "gz", axis=0, tiled=True)
    gathered = lax.all_to_all(
        jnp.broadcast_to(mentions[None], (x_size, rows, width)), "gx", 0, 0, tiled=True
    )

    slot_live = jnp.arange(slot_max, dtype=jnp.int32)[None, :] < list_lengths[:, None]
    owner = block_lists // col_count
    owner_ids = jnp.arange(z_size * x_size, dtype=jnp.int32)
    listed = jnp.any(
        slot_live[:, :, None] & (owner[:, :, None] == owner_ids[None, None, :]), axis=1
    )
    listed = listed.reshape(groups, z_size, x_size).transpose(2, 1, 0).astype(f32)
    listed = jnp.repeat(listed, block_rows, axis=2)
    slots = gold_slot.reshape(groups, block_rows)
    slot_ids = jnp.arange(slot_max, dtype=jnp.int32)
    gold_owner = jnp.sum(
        jnp.where(slots[:, :, None] == slot_ids[None, None, :], owner[:, None, :], 0), axis=2
    ).reshape(1, rows)
    x_ids = jnp.arange(x_size, dtype=jnp.int32)[:, None]
    gold = jnp.where(
        gold_owner % x_size == x_ids,
        gold_owner // x_size * block_rows + gold_row.reshape(1, rows),
        -1,
    ).astype(f32)
    meta = jnp.concatenate(
        [listed, gold[:, None, :], jnp.zeros((x_size, META_ROWS - z_size - 1, rows), f32)], axis=1
    )
    meta = lax.all_to_all(meta, "gx", 0, 0, tiled=True)

    tile = lambda *shape: pl.BlockSpec((1,) + shape, lambda j: (j, 0, 0))
    whole = pl.BlockSpec((types, width), lambda j: (0, 0))
    raw_dot, stats = pl.pallas_call(
        scores_kernel,
        grid=(x_size,),
        in_specs=[smem, tile(rows, width), whole, tile(META_ROWS, rows)],
        out_specs=[
            tile(types, rows),
            pl.BlockSpec((x_size, STAT_ROWS, x_size * rows), lambda j: (0, 0, 0)),
        ],
        out_shape=[
            jax.ShapeDtypeStruct((x_size, types, rows), f32),
            jax.ShapeDtypeStruct((x_size, STAT_ROWS, x_size * rows), f32),
        ],
        compiler_params=params(),
        name="scores",
    )(logit_scale, gathered, table, meta)
    stats = lax.all_to_all(stats, "gx", 0, 0, tiled=True)
    grads, type_part, scale_part = pl.pallas_call(
        grads_kernel,
        grid=(x_size,),
        in_specs=[
            smem,
            tile(types, rows),
            tile(META_ROWS, rows),
            pl.BlockSpec((x_size, STAT_ROWS, rows), lambda j: (0, 0, j)),
            tile(rows, width),
        ],
        out_specs=[
            tile(types, rows),
            whole,
            pl.BlockSpec((1, 128), lambda j: (0, 0)),
        ],
        out_shape=[
            jax.ShapeDtypeStruct((x_size, types, rows), bf16),
            jax.ShapeDtypeStruct((types, width), bf16),
            jax.ShapeDtypeStruct((1, 128), f32),
        ],
        scratch_shapes=[pltpu.VMEM((types, width), f32), pltpu.VMEM((1, rows), f32)],
        compiler_params=params(),
        name="grads",
    )(logit_scale, raw_dot, meta, stats, gathered)
    type_grad = lax.psum_scatter(type_part, "gz", scatter_dimension=0, tiled=True)
    mention_part = pl.pallas_call(
        mention_kernel,
        grid=(x_size,),
        in_specs=[smem, tile(types, rows), whole],
        out_specs=tile(rows, width),
        out_shape=jax.ShapeDtypeStruct((x_size, rows, width), bf16),
        compiler_params=params(),
        name="mention_part",
    )(logit_scale, grads, table)
    mention_grad = lax.all_to_all(mention_part, "gx", 0, 0, tiled=True)
    mention_grad = jnp.sum(mention_grad, axis=0, dtype=f32).astype(bf16)
    scale_parts = lax.all_to_all(
        jnp.broadcast_to(scale_part[None], (devices, 1, 128)), ("gz", "gx", "gy"), 0, 0, tiled=True
    )
    scale_grad = (jnp.sum(scale_parts[:, 0, 0]) / (rows * devices)).reshape(1)
    new_table, new_first, new_second = adam_rows(
        type_table, adam_m, adam_v, type_grad.astype(f32)
    )
    return (new_table, new_first, new_second, mention_grad, scale_grad)


def solution(mesh):
    gx, gy = mesh.devices.shape
    split = Mesh(mesh.devices.reshape(gx // X_SIZE, X_SIZE, gy), ("gz", "gx", "gy"))
    axes = ("gz", "gx", "gy")
    rows = P(axes, None)
    return jax.shard_map(
        per_device,
        mesh=split,
        in_specs=(rows, rows, rows, rows, P(), rows, P(axes), P(axes), P(axes)),
        out_specs=(rows, rows, rows, rows, P()),
        check_vma=False,
    )
```

```python
import jax
import jax.numpy as jnp
from jax import lax
from jax.experimental import pallas as pl
from jax.experimental.pallas import tpu as pltpu
from jax.sharding import Mesh, PartitionSpec as P

beta_one = 0.9
beta_two = 0.999
learn_rate = 0.02
adam_eps = 1e-08
first_fix = 0.9999734386011124
second_fix = 0.09520785288629038

X_SIZE = 4
Z_SIZE = 8
BLOCK = 128
LOW = -1e30
META_ROWS = 16
SLOTS = 16
STAT_ROWS = 8
OFFSETS = (0, -1, 1, -2, 2, -3, 3, 4)
f32 = jnp.float32
bf16 = jnp.bfloat16


def pack_kernel(cols, list_ref, len_ref, slot_ref, row_ref, m_ref, out_ref):
    rows, width = m_ref.shape
    out_ref[0, 0:rows, :] = m_ref[...]
    first = lax.broadcasted_iota(jnp.int32, (1, rows), 1) < BLOCK
    slot = slot_ref[...]
    gold = jnp.zeros((1, rows), f32)
    parts = []
    for k in range(SLOTS):
        ids = [
            jnp.where(k < len_ref[g], lax.div(list_ref[g, k], cols), -1).astype(f32)
            for g in range(2)
        ]
        part = jnp.where(first, ids[0], ids[1])
        gold = gold + jnp.where(slot == k, part, 0.0)
        parts.append(part)
    parts += [gold, row_ref[...].astype(f32)]
    per_row = width // rows
    lines = [
        jnp.concatenate(parts[i : i + per_row], axis=1) for i in range(0, len(parts), per_row)
    ]
    lines.append(jnp.zeros((META_ROWS - len(lines), width), f32))
    out_ref[0, rows : rows + META_ROWS, :] = jnp.concatenate(lines, axis=0).astype(bf16)


def read_meta(m_ref, rows):
    meta = m_ref[0, rows : rows + META_ROWS, :].astype(f32)
    per_row = meta.shape[1] // rows
    parts = [
        meta[i // per_row : i // per_row + 1, (i % per_row) * rows : (i % per_row + 1) * rows]
        for i in range(SLOTS + 2)
    ]
    owners = jnp.concatenate(parts[:SLOTS], axis=0)
    return owners, parts[SLOTS], parts[SLOTS + 1].astype(jnp.int32)


def owner_of(place_ref, offset):
    line = lax.rem(place_ref[0] + (offset + Z_SIZE), Z_SIZE)
    return line, (line * X_SIZE + place_ref[1]).astype(f32)


def listed_in(owners, owner):
    return jnp.max(jnp.where(owners == owner, 1.0, 0.0), axis=0, keepdims=True) > 0.0


def gather_tile(t_refs, tile_ref):
    at = 0
    for ref in t_refs:
        n = ref.shape[0]
        tile_ref[at : at + n, :] = ref[...]
        at += n


def scores_kernel(factor_ref, place_ref, m_ref, *refs):
    t_refs, (raw_ref, stat_ref, tile_ref) = refs[:-3], refs[-3:]
    step = pl.program_id(0)
    factor = factor_ref[0]
    rows = m_ref.shape[1] - META_ROWS
    pl.when(step == 0)(lambda: gather_tile(t_refs, tile_ref))
    raw_ref[0] = lax.dot_general(
        tile_ref[...], m_ref[0, 0:rows, :], (((1,), (1,)), ((), ())), preferred_element_type=f32
    )
    owners, gold_owner, gold_row = read_meta(m_ref, rows)
    ids = lax.broadcasted_iota(jnp.int32, (BLOCK, rows), 0)
    top = jnp.full((1, rows), LOW, f32)
    gold_raw = jnp.zeros((1, rows), f32)
    lives = []
    for c, offset in enumerate(OFFSETS):
        _, owner = owner_of(place_ref, offset)
        lives.append(listed_in(owners, owner))
        raw = raw_ref[0, c * BLOCK : (c + 1) * BLOCK, :]
        part = jnp.max(factor * raw, axis=0, keepdims=True)
        top = jnp.maximum(top, jnp.where(lives[c], part, LOW))
        gold = jnp.where(gold_owner == owner, gold_row, -1)
        gold_raw = gold_raw + jnp.sum(jnp.where(ids == gold, raw, 0.0), axis=0, keepdims=True)
    total = jnp.zeros((1, rows), f32)
    mass = jnp.zeros((1, rows), f32)
    for c in range(len(OFFSETS)):
        raw = raw_ref[0, c * BLOCK : (c + 1) * BLOCK, :]
        weights = jnp.where(lives[c], jnp.exp(factor * raw - top), 0.0)
        total = total + jnp.sum(weights, axis=0, keepdims=True)
        mass = mass + jnp.sum(weights * raw, axis=0, keepdims=True)
    stat = jnp.concatenate(
        [top, total, mass, gold_raw, jnp.zeros((STAT_ROWS - 4, rows), f32)], axis=0
    )
    for d in range(stat_ref.shape[0]):
        stat_ref[d, :, pl.ds(pl.multiple_of(step * rows, BLOCK), rows)] = stat


def grads_kernel(
    factor_ref, place_ref, raw_ref, stat_ref, m_ref, g_ref, type_ref, scale_ref, acc_ref, sum_ref
):
    step = pl.program_id(0)
    factor = factor_ref[0]
    rows = m_ref.shape[1] - META_ROWS
    tops = stat_ref[:, 0, :]
    top = jnp.max(tops, axis=0, keepdims=True)
    share = jnp.exp(tops - top)
    total = jnp.sum(stat_ref[:, 1, :] * share, axis=0, keepdims=True)
    log_total = top + jnp.log(total)
    mass = jnp.sum(stat_ref[:, 2, :] * share, axis=0, keepdims=True)
    scale = mass / total - jnp.sum(stat_ref[:, 3, :], axis=0, keepdims=True)
    owners, gold_owner, gold_row = read_meta(m_ref, rows)
    ids = lax.broadcasted_iota(jnp.int32, (BLOCK, rows), 0)
    for c, offset in enumerate(OFFSETS):
        _, owner = owner_of(place_ref, offset)
        live = listed_in(owners, owner)
        raw = raw_ref[0, c * BLOCK : (c + 1) * BLOCK, :]
        weights = jnp.where(live, jnp.exp(factor * raw - log_total), 0.0)
        gold = jnp.where(gold_owner == owner, gold_row, -1)
        grad = weights - jnp.where(ids == gold, 1.0, 0.0)
        g_ref[0, c * BLOCK : (c + 1) * BLOCK, :] = grad.astype(bf16)
    part = jnp.dot(g_ref[0], m_ref[0, 0:rows, :], preferred_element_type=f32)

    @pl.when(step == 0)
    def _():
        acc_ref[...] = part
        sum_ref[...] = scale

    @pl.when(step > 0)
    def _():
        acc_ref[...] += part
        sum_ref[...] += scale

    @pl.when(step == pl.num_programs(0) - 1)
    def _():
        for c, offset in enumerate(OFFSETS):
            line, _ = owner_of(place_ref, offset)
            type_ref[line] = (factor * acc_ref[c * BLOCK : (c + 1) * BLOCK, :]).astype(bf16)
        scale_ref[...] = jnp.broadcast_to(
            jnp.sum(sum_ref[...], axis=1, keepdims=True), scale_ref.shape
        )


def mention_kernel(factor_ref, scale_ref, g_ref, *refs):
    t_refs, (out_ref, scale_out_ref, tile_ref) = refs[:-3], refs[-3:]

    @pl.when(pl.program_id(0) == 0)
    def _():
        gather_tile(t_refs, tile_ref)
        scale_out_ref[...] = scale_ref[...]

    part = lax.dot_general(
        g_ref[0], tile_ref[...], (((0,), (0,)), ((), ())), preferred_element_type=f32
    )
    out_ref[0] = (factor_ref[0] * part).astype(bf16)


def adam_kernel(part_ref, table_ref, m_ref, v_ref, table_out, m_out, v_out):
    grad = part_ref[0].astype(f32)
    for z in range(1, part_ref.shape[0]):
        grad = grad + part_ref[z].astype(f32)
    moment_one = beta_one * m_ref[...] + (1.0 - beta_one) * grad
    moment_two = beta_two * v_ref[...] + (1.0 - beta_two) * grad * grad
    table_out[...] = table_ref[...] - learn_rate * (moment_one / first_fix) / (
        jnp.sqrt(moment_two / second_fix) + adam_eps
    )
    m_out[...] = moment_one
    v_out[...] = moment_two


def params():
    return pltpu.CompilerParams(
        dimension_semantics=("arbitrary",), vmem_limit_bytes=40 * 1024 * 1024
    )


def shifted(array, axis, size, by):
    return lax.ppermute(array, axis, [(i, (i + by) % size) for i in range(size)])


def ring_gather(block):
    half = block.shape[0] // 2
    ups, downs = [block], [block]
    for _ in range(3):
        ups.append(shifted(ups[-1], "gz", Z_SIZE, 1))
        downs.append(shifted(downs[-1], "gz", Z_SIZE, -1))
    far = [
        shifted(ups[-1][:half], "gz", Z_SIZE, 1),
        shifted(downs[-1][half:], "gz", Z_SIZE, -1),
    ]
    return [block, ups[1], downs[1], ups[2], downs[2], ups[3], downs[3]] + far


def doubled(value, axis, size):
    by = 1
    while by < size:
        value = value + lax.ppermute(value, axis, [(i, i ^ by) for i in range(size)])
        by *= 2
    return value


def per_device(
    mentions,
    type_table,
    adam_m,
    adam_v,
    logit_scale,
    block_lists,
    list_lengths,
    gold_slot,
    gold_row,
):
    cols = lax.axis_size("gy")
    devices = Z_SIZE * X_SIZE * cols
    block_rows, width = type_table.shape
    rows = mentions.shape[0]
    sent_rows = rows + META_ROWS
    types = Z_SIZE * block_rows
    smem = pl.BlockSpec(memory_space=pltpu.SMEM)
    place = jnp.stack([lax.axis_index("gz"), lax.axis_index("gx")]).astype(jnp.int32)

    def tile(*shape):
        return pl.BlockSpec((1,) + shape, lambda j: (j, 0, 0))

    def whole(*shape):
        return pl.BlockSpec(shape, lambda j: (0,) * len(shape))

    blocks = ring_gather(type_table.astype(bf16))
    block_specs = [whole(b.shape[0], width) for b in blocks]
    packed = pl.pallas_call(
        lambda *refs: pack_kernel(cols, *refs),
        grid=(X_SIZE,),
        in_specs=[smem, smem, whole(1, rows), whole(1, rows), whole(rows, width)],
        out_specs=tile(sent_rows, width),
        out_shape=jax.ShapeDtypeStruct((X_SIZE, sent_rows, width), bf16),
        compiler_params=params(),
        name="pack",
    )(block_lists, list_lengths, gold_slot.reshape(1, rows), gold_row.reshape(1, rows), mentions)
    gathered = lax.all_to_all(packed, "gx", 0, 0, tiled=True)

    raw_dot, stats = pl.pallas_call(
        scores_kernel,
        grid=(X_SIZE,),
        in_specs=[smem, smem, tile(sent_rows, width)] + block_specs,
        out_specs=[tile(types, rows), whole(X_SIZE, STAT_ROWS, X_SIZE * rows)],
        out_shape=[
            jax.ShapeDtypeStruct((X_SIZE, types, rows), f32),
            jax.ShapeDtypeStruct((X_SIZE, STAT_ROWS, X_SIZE * rows), f32),
        ],
        scratch_shapes=[pltpu.VMEM((types, width), bf16)],
        compiler_params=params(),
        name="scores",
    )(logit_scale, place, gathered, *blocks)
    stats = lax.all_to_all(stats, "gx", 0, 0, tiled=True)
    grads, type_part, scale_part = pl.pallas_call(
        grads_kernel,
        grid=(X_SIZE,),
        in_specs=[
            smem,
            smem,
            tile(types, rows),
            pl.BlockSpec((X_SIZE, STAT_ROWS, rows), lambda j: (0, 0, j)),
            tile(sent_rows, width),
        ],
        out_specs=[tile(types, rows), whole(Z_SIZE, block_rows, width), whole(1, 128)],
        out_shape=[
            jax.ShapeDtypeStruct((X_SIZE, types, rows), bf16),
            jax.ShapeDtypeStruct((Z_SIZE, block_rows, width), bf16),
            jax.ShapeDtypeStruct((1, 128), f32),
        ],
        scratch_shapes=[pltpu.VMEM((types, width), f32), pltpu.VMEM((1, rows), f32)],
        compiler_params=params(),
        name="grads",
    )(logit_scale, place, raw_dot, stats, gathered)
    type_parts = lax.all_to_all(type_part, "gz", 0, 0, tiled=True)
    mention_part, scale_part = pl.pallas_call(
        mention_kernel,
        grid=(X_SIZE,),
        in_specs=[smem, whole(1, 128), tile(types, rows)] + block_specs,
        out_specs=[tile(rows, width), whole(1, 128)],
        out_shape=[
            jax.ShapeDtypeStruct((X_SIZE, rows, width), bf16),
            jax.ShapeDtypeStruct((1, 128), f32),
        ],
        scratch_shapes=[pltpu.VMEM((types, width), bf16)],
        compiler_params=params(),
        name="mention_part",
    )(logit_scale, scale_part, grads, *blocks)
    mention_grad = lax.psum_scatter(
        mention_part.reshape(X_SIZE * rows, width), "gx", scatter_dimension=0, tiled=True
    )
    scale_sum = doubled(doubled(scale_part, "gz", Z_SIZE), "gy", cols)
    scale_grad = (scale_sum[0, 0] / (rows * devices)).reshape(1)
    slab = block_rows // 4
    row_tile = pl.BlockSpec((slab, width), lambda j: (j, 0))
    new_table, new_first, new_second = pl.pallas_call(
        adam_kernel,
        grid=(block_rows // slab,),
        in_specs=[pl.BlockSpec((Z_SIZE, slab, width), lambda j: (0, j, 0))] + [row_tile] * 3,
        out_specs=[row_tile] * 3,
        out_shape=[jax.ShapeDtypeStruct((block_rows, width), f32)] * 3,
        compiler_params=params(),
        name="adam",
    )(type_parts, type_table, adam_m, adam_v)
    return (new_table, new_first, new_second, mention_grad, scale_grad)


def solution(mesh):
    gx, gy = mesh.devices.shape
    split = Mesh(mesh.devices.reshape(gx // X_SIZE, X_SIZE, gy), ("gz", "gx", "gy"))
    axes = ("gz", "gx", "gy")
    rows = P(axes, None)
    return jax.shard_map(
        per_device,
        mesh=split,
        in_specs=(rows, rows, rows, rows, P(), rows, P(axes), P(axes), P(axes)),
        out_specs=(rows, rows, rows, rows, P()),
        check_vma=False,
    )
```

```python
import jax
import jax.numpy as jnp
from jax import lax
from jax.experimental import pallas as pl
from jax.experimental.pallas import tpu as pltpu
from jax.sharding import Mesh, PartitionSpec as P

beta_one = 0.9
beta_two = 0.999
learn_rate = 0.02
adam_eps = 1e-08
first_fix = 0.9999734386011124
second_fix = 0.09520785288629038

X_SIZE = 4
Z_SIZE = 8
BLOCK = 128
LOW = -1e30
META_ROWS = 16
SLOTS = 16
STAT_ROWS = 8
f32 = jnp.float32
bf16 = jnp.bfloat16


def pack_kernel(
    cols, list_hbm, len_hbm, slot_hbm, row_hbm, m_hbm, t_hbm, m_out, t_out, list_ref, len_ref, slot_ref, row_ref, t_ref, sems
):
    rows, width = m_hbm.shape
    pairs = [
        (list_hbm, list_ref),
        (len_hbm, len_ref),
        (slot_hbm, slot_ref),
        (row_hbm, row_ref),
        (t_hbm, t_ref),
        (m_hbm, m_out.at[pl.ds(0, rows), :]),
    ]
    copies = [pltpu.make_async_copy(src, dst, sems.at[i]) for i, (src, dst) in enumerate(pairs)]
    for copy in copies:
        copy.start()
    for copy in copies[:4]:
        copy.wait()
    owners = lax.div(list_ref[...], cols).astype(f32)
    lens = len_ref[...]
    first = lax.broadcasted_iota(jnp.int32, (1, rows), 1) < BLOCK
    length = jnp.where(first, lens[:, 0:1], lens[:, 1:2])
    slot = slot_ref[...]
    gold = jnp.zeros((1, rows), f32)
    parts = []
    for k in range(SLOTS):
        owner = jnp.where(first, owners[0:1, k : k + 1], owners[1:2, k : k + 1])
        gold = gold + jnp.where(slot == k, owner, 0.0)
        parts.append(jnp.where(length > k, owner, -1.0))
    parts += [gold, row_ref[...].astype(f32)]
    per_row = width // rows
    lines = [
        jnp.concatenate(parts[i : i + per_row], axis=1) for i in range(0, len(parts), per_row)
    ]
    lines.append(jnp.zeros((META_ROWS - len(lines), width), f32))
    m_out[rows : rows + META_ROWS, :] = jnp.concatenate(lines, axis=0).astype(bf16)
    copies[4].wait()
    table = t_ref[...].astype(bf16)
    for z in range(t_out.shape[0]):
        t_out[z] = table
    copies[5].wait()


def read_meta(m_ref, rows):
    meta = m_ref[0, rows : rows + META_ROWS, :].astype(f32)
    per_row = meta.shape[1] // rows
    parts = [
        meta[i // per_row : i // per_row + 1, (i % per_row) * rows : (i % per_row + 1) * rows]
        for i in range(SLOTS + 2)
    ]
    owners = jnp.concatenate(parts[:SLOTS], axis=0)
    return owners, parts[SLOTS], parts[SLOTS + 1].astype(jnp.int32)


def listed_in(owners, owner):
    return jnp.max(jnp.where(owners == owner, 1.0, 0.0), axis=0, keepdims=True) > 0.0


def owner_at(place_ref, line):
    return (line * X_SIZE + place_ref[0]).astype(f32)


def scores_kernel(factor_ref, place_ref, m_ref, t_ref, raw_ref, stat_ref):
    step = pl.program_id(0)
    factor = factor_ref[0]
    rows = m_ref.shape[1] - META_ROWS
    raw_ref[0] = lax.dot_general(
        t_ref[...], m_ref[0, 0:rows, :], (((1,), (1,)), ((), ())), preferred_element_type=f32
    )
    owners, gold_owner, gold_row = read_meta(m_ref, rows)
    ids = lax.broadcasted_iota(jnp.int32, (BLOCK, rows), 0)
    top = jnp.full((1, rows), LOW, f32)
    gold_raw = jnp.zeros((1, rows), f32)
    lives = []
    for c in range(Z_SIZE):
        owner = owner_at(place_ref, c)
        lives.append(listed_in(owners, owner))
        raw = raw_ref[0, c * BLOCK : (c + 1) * BLOCK, :]
        part = jnp.max(factor * raw, axis=0, keepdims=True)
        top = jnp.maximum(top, jnp.where(lives[c], part, LOW))
        gold = jnp.where(gold_owner == owner, gold_row, -1)
        gold_raw = gold_raw + jnp.sum(jnp.where(ids == gold, raw, 0.0), axis=0, keepdims=True)
    total = jnp.zeros((1, rows), f32)
    mass = jnp.zeros((1, rows), f32)
    for c in range(Z_SIZE):
        raw = raw_ref[0, c * BLOCK : (c + 1) * BLOCK, :]
        weights = jnp.where(lives[c], jnp.exp(factor * raw - top), 0.0)
        total = total + jnp.sum(weights, axis=0, keepdims=True)
        mass = mass + jnp.sum(weights * raw, axis=0, keepdims=True)
    stat = jnp.concatenate(
        [top, total, mass, gold_raw, jnp.zeros((STAT_ROWS - 4, rows), f32)], axis=0
    )
    for d in range(stat_ref.shape[0]):
        stat_ref[d, :, pl.ds(pl.multiple_of(step * rows, BLOCK), rows)] = stat


def grads_kernel(
    factor_ref, place_ref, raw_ref, stat_ref, m_ref, t_ref, mention_ref, type_ref, scale_ref, g_ref, acc_ref, sum_ref
):
    step = pl.program_id(0)
    factor = factor_ref[0]
    rows = m_ref.shape[1] - META_ROWS
    tops = stat_ref[:, 0, :]
    top = jnp.max(tops, axis=0, keepdims=True)
    share = jnp.exp(tops - top)
    total = jnp.sum(stat_ref[:, 1, :] * share, axis=0, keepdims=True)
    log_total = top + jnp.log(total)
    mass = jnp.sum(stat_ref[:, 2, :] * share, axis=0, keepdims=True)
    scale = mass / total - jnp.sum(stat_ref[:, 3, :], axis=0, keepdims=True)
    owners, gold_owner, gold_row = read_meta(m_ref, rows)
    ids = lax.broadcasted_iota(jnp.int32, (BLOCK, rows), 0)
    for c in range(Z_SIZE):
        owner = owner_at(place_ref, c)
        live = listed_in(owners, owner)
        raw = raw_ref[0, c * BLOCK : (c + 1) * BLOCK, :]
        weights = jnp.where(live, jnp.exp(factor * raw - log_total), 0.0)
        gold = jnp.where(gold_owner == owner, gold_row, -1)
        grad = weights - jnp.where(ids == gold, 1.0, 0.0)
        g_ref[c * BLOCK : (c + 1) * BLOCK, :] = grad.astype(bf16)
    part = jnp.dot(g_ref[...], m_ref[0, 0:rows, :], preferred_element_type=f32)

    @pl.when(step == 0)
    def _():
        acc_ref[...] = part
        sum_ref[...] = scale

    @pl.when(step > 0)
    def _():
        acc_ref[...] += part
        sum_ref[...] += scale

    mention = lax.dot_general(
        g_ref[...], t_ref[...], (((0,), (0,)), ((), ())), preferred_element_type=f32
    )
    mention_ref[0] = (factor * mention).astype(bf16)

    @pl.when(step == pl.num_programs(0) - 1)
    def _():
        type_ref[...] = (factor * acc_ref[...]).astype(bf16)
        scale_ref[...] = jnp.broadcast_to(
            jnp.sum(sum_ref[...], axis=1, keepdims=True), scale_ref.shape
        )


def adam_kernel(part_ref, table_ref, m_ref, v_ref, table_out, m_out, v_out):
    grad = part_ref[0].astype(f32)
    for z in range(1, part_ref.shape[0]):
        grad = grad + part_ref[z].astype(f32)
    moment_one = beta_one * m_ref[...] + (1.0 - beta_one) * grad
    moment_two = beta_two * v_ref[...] + (1.0 - beta_two) * grad * grad
    table_out[...] = table_ref[...] - learn_rate * (moment_one / first_fix) / (
        jnp.sqrt(moment_two / second_fix) + adam_eps
    )
    m_out[...] = moment_one
    v_out[...] = moment_two


def params(mib=52):
    return pltpu.CompilerParams(vmem_limit_bytes=mib * 1024 * 1024)


def doubled(value, axis, size):
    by = 1
    while by < size:
        value = value + lax.ppermute(value, axis, [(i, i ^ by) for i in range(size)])
        by *= 2
    return value


def per_device(
    mentions,
    type_table,
    adam_m,
    adam_v,
    logit_scale,
    block_lists,
    list_lengths,
    gold_slot,
    gold_row,
):
    cols = lax.axis_size("gy")
    devices = Z_SIZE * X_SIZE * cols
    block_rows, width = type_table.shape
    rows = mentions.shape[0]
    sent_rows = rows + META_ROWS
    types = Z_SIZE * block_rows
    smem = pl.BlockSpec(memory_space=pltpu.SMEM)
    hbm = pl.BlockSpec(memory_space=pltpu.HBM)
    place = lax.axis_index("gx").reshape(1).astype(jnp.int32)

    def tile(*shape):
        return pl.BlockSpec((1,) + shape, lambda j: (j, 0, 0))

    def whole(*shape):
        return pl.BlockSpec(shape, lambda j: (0,) * len(shape))

    packed, copies = pl.pallas_call(
        lambda *refs: pack_kernel(cols, *refs),
        in_specs=[hbm] * 6,
        out_shape=[
            jax.ShapeDtypeStruct((sent_rows, width), bf16),
            jax.ShapeDtypeStruct((Z_SIZE, block_rows, width), bf16),
        ],
        scratch_shapes=[
            pltpu.VMEM((2, SLOTS), jnp.int32),
            pltpu.VMEM((1, 2), jnp.int32),
            pltpu.VMEM((1, rows), jnp.int32),
            pltpu.VMEM((1, rows), jnp.int32),
            pltpu.VMEM((block_rows, width), f32),
            pltpu.SemaphoreType.DMA((6,)),
        ],
        compiler_params=params(60),
        name="pack",
    )(
        block_lists,
        list_lengths.reshape(1, 2),
        gold_slot.reshape(1, rows),
        gold_row.reshape(1, rows),
        mentions,
        type_table,
    )
    table = lax.all_to_all(copies, "gz", 0, 0, tiled=True).reshape(types, width)
    gathered = lax.all_gather(packed, "gx", axis=0, tiled=True)
    gathered = gathered.reshape(X_SIZE, sent_rows, width)

    raw_dot, stats = pl.pallas_call(
        scores_kernel,
        grid=(X_SIZE,),
        in_specs=[smem, smem, tile(sent_rows, width), whole(types, width)],
        out_specs=[tile(types, rows), whole(X_SIZE, STAT_ROWS, X_SIZE * rows)],
        out_shape=[
            jax.ShapeDtypeStruct((X_SIZE, types, rows), f32),
            jax.ShapeDtypeStruct((X_SIZE, STAT_ROWS, X_SIZE * rows), f32),
        ],
        compiler_params=params(),
        name="scores",
    )(logit_scale, place, gathered, table)
    stats = lax.all_to_all(stats, "gx", 0, 0, tiled=True)
    mention_part, type_part, scale_part = pl.pallas_call(
        grads_kernel,
        grid=(X_SIZE,),
        in_specs=[
            smem,
            smem,
            tile(types, rows),
            pl.BlockSpec((X_SIZE, STAT_ROWS, rows), lambda j: (0, 0, j)),
            tile(sent_rows, width),
            whole(types, width),
        ],
        out_specs=[tile(rows, width), whole(types, width), whole(1, 128)],
        out_shape=[
            jax.ShapeDtypeStruct((X_SIZE, rows, width), bf16),
            jax.ShapeDtypeStruct((types, width), bf16),
            jax.ShapeDtypeStruct((1, 128), f32),
        ],
        scratch_shapes=[
            pltpu.VMEM((types, rows), bf16),
            pltpu.VMEM((types, width), f32),
            pltpu.VMEM((1, rows), f32),
        ],
        compiler_params=params(),
        name="grads",
    )(logit_scale, place, raw_dot, stats, gathered, table)
    type_parts = lax.all_to_all(
        type_part.reshape(Z_SIZE, block_rows, width), "gz", 0, 0, tiled=True
    )
    mention_grad = lax.psum_scatter(
        mention_part.reshape(X_SIZE * rows, width), "gx", scatter_dimension=0, tiled=True
    )
    scale_sum = doubled(scale_part, "gy", cols) + 0.0 * type_parts[0, 0:1, 0:128].astype(f32)
    scale_sums = lax.all_to_all(
        jnp.broadcast_to(scale_sum[None], (Z_SIZE, 1, 128)), "gz", 0, 0, tiled=True
    )
    scale_grad = (jnp.sum(scale_sums[:, 0, 0]) / (rows * devices)).reshape(1)
    slab = block_rows // 4
    row_tile = pl.BlockSpec((slab, width), lambda j: (j, 0))
    new_table, new_first, new_second = pl.pallas_call(
        adam_kernel,
        grid=(block_rows // slab,),
        in_specs=[pl.BlockSpec((Z_SIZE, slab, width), lambda j: (0, j, 0))] + [row_tile] * 3,
        out_specs=[row_tile] * 3,
        out_shape=[jax.ShapeDtypeStruct((block_rows, width), f32)] * 3,
        compiler_params=params(16),
        name="adam",
    )(type_parts, type_table, adam_m, adam_v)
    return (new_table, new_first, new_second, mention_grad, scale_grad)


def solution(mesh):
    gx, gy = mesh.devices.shape
    split = Mesh(mesh.devices.reshape(gx // X_SIZE, X_SIZE, gy), ("gz", "gx", "gy"))
    axes = ("gz", "gx", "gy")
    rows = P(axes, None)
    return jax.shard_map(
        per_device,
        mesh=split,
        in_specs=(rows, rows, rows, rows, P(), rows, P(axes), P(axes), P(axes)),
        out_specs=(rows, rows, rows, rows, P()),
        check_vma=False,
    )
```

```python
import jax
import jax.numpy as jnp
from jax import lax
from jax.experimental import pallas as pl
from jax.experimental.pallas import tpu as pltpu
from jax.sharding import Mesh, PartitionSpec as P

beta_one = 0.9
beta_two = 0.999
learn_rate = 0.02
adam_eps = 1e-08
first_fix = 0.9999734386011124
second_fix = 0.09520785288629038

X_SIZE = 4
Z_SIZE = 8
BLOCK = 128
LOW = -1e30
META_ROWS = 16
SLOTS = 16
STAT_ROWS = 8
f32 = jnp.float32
bf16 = jnp.bfloat16


def pack_kernel(
    cols, list_hbm, len_hbm, slot_hbm, row_hbm, m_hbm, out_ref, list_ref, len_ref, slot_ref, row_ref, sems
):
    rows, width = m_hbm.shape
    pairs = [(list_hbm, list_ref), (len_hbm, len_ref), (slot_hbm, slot_ref), (row_hbm, row_ref)]
    pairs += [(m_hbm, out_ref.at[x, pl.ds(0, rows), :]) for x in range(X_SIZE)]
    copies = [pltpu.make_async_copy(src, dst, sems.at[i]) for i, (src, dst) in enumerate(pairs)]
    for copy in copies:
        copy.start()
    for copy in copies[:4]:
        copy.wait()
    owners = lax.div(list_ref[...], cols).astype(f32)
    lens = len_ref[...]
    first = lax.broadcasted_iota(jnp.int32, (1, rows), 1) < BLOCK
    length = jnp.where(first, lens[:, 0:1], lens[:, 1:2])
    slot = slot_ref[...]
    gold = jnp.zeros((1, rows), f32)
    parts = []
    for k in range(SLOTS):
        owner = jnp.where(first, owners[0:1, k : k + 1], owners[1:2, k : k + 1])
        gold = gold + jnp.where(slot == k, owner, 0.0)
        parts.append(jnp.where(length > k, owner, -1.0))
    parts += [gold, row_ref[...].astype(f32)]
    per_row = width // rows
    lines = [
        jnp.concatenate(parts[i : i + per_row], axis=1) for i in range(0, len(parts), per_row)
    ]
    lines.append(jnp.zeros((META_ROWS - len(lines), width), f32))
    meta = jnp.concatenate(lines, axis=0).astype(bf16)
    for x in range(X_SIZE):
        out_ref[x, rows : rows + META_ROWS, :] = meta
    for copy in copies[4:]:
        copy.wait()


def read_meta(m_ref, rows):
    meta = m_ref[0, rows : rows + META_ROWS, :].astype(f32)
    per_row = meta.shape[1] // rows
    parts = [
        meta[i // per_row : i // per_row + 1, (i % per_row) * rows : (i % per_row + 1) * rows]
        for i in range(SLOTS + 2)
    ]
    owners = jnp.concatenate(parts[:SLOTS], axis=0)
    return owners, parts[SLOTS], parts[SLOTS + 1].astype(jnp.int32)


def listed_in(owners, owner):
    return jnp.max(jnp.where(owners == owner, 1.0, 0.0), axis=0, keepdims=True) > 0.0


def owner_at(place_ref, line):
    return (line * X_SIZE + place_ref[0]).astype(f32)


def scores_kernel(factor_ref, place_ref, m_ref, t_ref, exp_ref, stat_ref, raw_ref):
    step = pl.program_id(0)
    factor = factor_ref[0]
    rows = m_ref.shape[1] - META_ROWS
    raw_ref[...] = lax.dot_general(
        t_ref[...], m_ref[0, 0:rows, :], (((1,), (1,)), ((), ())), preferred_element_type=f32
    )
    owners, gold_owner, gold_row = read_meta(m_ref, rows)
    ids = lax.broadcasted_iota(jnp.int32, (BLOCK, rows), 0)
    top = jnp.full((1, rows), LOW, f32)
    gold_raw = jnp.zeros((1, rows), f32)
    lives = []
    for c in range(Z_SIZE):
        owner = owner_at(place_ref, c)
        lives.append(listed_in(owners, owner))
        raw = raw_ref[c * BLOCK : (c + 1) * BLOCK, :]
        top = jnp.maximum(top, jnp.where(lives[c], jnp.max(raw, axis=0, keepdims=True), LOW))
        gold = jnp.where(gold_owner == owner, gold_row, -1)
        gold_raw = gold_raw + jnp.sum(jnp.where(ids == gold, raw, 0.0), axis=0, keepdims=True)
    total = jnp.zeros((1, rows), f32)
    mass = jnp.zeros((1, rows), f32)
    for c in range(Z_SIZE):
        below = jnp.where(lives[c], top, -LOW)
        gap = raw_ref[c * BLOCK : (c + 1) * BLOCK, :] - below
        weights = jnp.exp(factor * gap)
        exp_ref[0, c * BLOCK : (c + 1) * BLOCK, :] = weights
        total = total + jnp.sum(weights, axis=0, keepdims=True)
        mass = mass + jnp.sum(weights * gap, axis=0, keepdims=True)
    stat = jnp.concatenate(
        [top, total, mass, gold_raw, jnp.zeros((STAT_ROWS - 4, rows), f32)], axis=0
    )
    for d in range(stat_ref.shape[0]):
        stat_ref[d, :, pl.ds(pl.multiple_of(step * rows, BLOCK), rows)] = stat


def grads_kernel(
    factor_ref, place_ref, exp_ref, stat_ref, m_ref, g_ref, type_ref, scale_ref, acc_ref, sum_ref
):
    step = pl.program_id(0)
    factor = factor_ref[0]
    rows = m_ref.shape[1] - META_ROWS
    tops = stat_ref[:, 0, :]
    sums = stat_ref[:, 1, :]
    top = jnp.max(tops, axis=0, keepdims=True)
    shares = jnp.exp(factor * (tops - top))
    total = jnp.sum(sums * shares, axis=0, keepdims=True)
    masses = stat_ref[:, 2, :] + sums * tops
    mass = jnp.sum(jnp.where(sums > 0.0, masses * shares, 0.0), axis=0, keepdims=True)
    scale = mass / total - jnp.sum(stat_ref[:, 3, :], axis=0, keepdims=True)
    ids = lax.broadcasted_iota(jnp.int32, (X_SIZE, rows), 0)
    own = jnp.max(jnp.where(ids == place_ref[0], tops, LOW), axis=0, keepdims=True)
    share = jnp.exp(factor * (own - top) - jnp.log(total))
    _, gold_owner, gold_row = read_meta(m_ref, rows)
    ids = lax.broadcasted_iota(jnp.int32, (BLOCK, rows), 0)
    for c in range(Z_SIZE):
        gold = jnp.where(gold_owner == owner_at(place_ref, c), gold_row, -1)
        weights = share * exp_ref[0, c * BLOCK : (c + 1) * BLOCK, :]
        grad = weights - jnp.where(ids == gold, 1.0, 0.0)
        g_ref[0, c * BLOCK : (c + 1) * BLOCK, :] = grad.astype(bf16)
    part = jnp.dot(g_ref[0], m_ref[0, 0:rows, :], preferred_element_type=f32)

    @pl.when(step == 0)
    def _():
        acc_ref[...] = part
        sum_ref[...] = scale

    @pl.when(step > 0)
    def _():
        acc_ref[...] += part
        sum_ref[...] += scale

    @pl.when(step == pl.num_programs(0) - 1)
    def _():
        type_ref[...] = (factor * acc_ref[...]).astype(bf16)
        scale_ref[...] = jnp.broadcast_to(
            jnp.sum(sum_ref[...], axis=1, keepdims=True), scale_ref.shape
        )


def mention_kernel(factor_ref, scale_ref, g_ref, t_ref, out_ref, scales_ref):
    part = lax.dot_general(
        g_ref[0], t_ref[...], (((0,), (0,)), ((), ())), preferred_element_type=f32
    )
    out_ref[0] = (factor_ref[0] * part).astype(bf16)

    @pl.when(pl.program_id(0) == 0)
    def _():
        scales_ref[...] = jnp.broadcast_to(scale_ref[...][None], scales_ref.shape)


def adam_rows(type_table, adam_m, adam_v, type_grad):
    moment_one = beta_one * adam_m + (1.0 - beta_one) * type_grad
    moment_two = beta_two * adam_v + (1.0 - beta_two) * type_grad * type_grad
    updated = type_table - learn_rate * (moment_one / first_fix) / (
        jnp.sqrt(moment_two / second_fix) + adam_eps
    )
    return (updated, moment_one, moment_two)


def params():
    return pltpu.CompilerParams(vmem_limit_bytes=60 * 1024 * 1024)


def per_device(
    mentions,
    type_table,
    adam_m,
    adam_v,
    logit_scale,
    block_lists,
    list_lengths,
    gold_slot,
    gold_row,
):
    cols = lax.axis_size("gy")
    devices = Z_SIZE * X_SIZE * cols
    block_rows, width = type_table.shape
    rows = mentions.shape[0]
    sent_rows = rows + META_ROWS
    types = Z_SIZE * block_rows
    smem = pl.BlockSpec(memory_space=pltpu.SMEM)
    hbm = pl.BlockSpec(memory_space=pltpu.HBM)
    place = lax.axis_index("gx").reshape(1).astype(jnp.int32)

    def tile(*shape):
        return pl.BlockSpec((1,) + shape, lambda j: (j, 0, 0))

    def whole(*shape):
        return pl.BlockSpec(shape, lambda j: (0,) * len(shape))

    table = lax.all_gather(type_table.astype(bf16), "gz", axis=0, tiled=True)
    packed = pl.pallas_call(
        lambda *refs: pack_kernel(cols, *refs),
        in_specs=[hbm] * 5,
        out_shape=jax.ShapeDtypeStruct((X_SIZE, sent_rows, width), bf16),
        scratch_shapes=[
            pltpu.VMEM((2, SLOTS), jnp.int32),
            pltpu.VMEM((1, 2), jnp.int32),
            pltpu.VMEM((1, rows), jnp.int32),
            pltpu.VMEM((1, rows), jnp.int32),
            pltpu.SemaphoreType.DMA((4 + X_SIZE,)),
        ],
        compiler_params=params(),
        name="pack",
    )(
        block_lists,
        list_lengths.reshape(1, 2),
        gold_slot.reshape(1, rows),
        gold_row.reshape(1, rows),
        mentions,
    )
    gathered = lax.all_to_all(packed, "gx", 0, 0, tiled=True)

    exps, stats = pl.pallas_call(
        scores_kernel,
        grid=(X_SIZE,),
        in_specs=[smem, smem, tile(sent_rows, width), whole(types, width)],
        out_specs=[tile(types, rows), whole(X_SIZE, STAT_ROWS, X_SIZE * rows)],
        out_shape=[
            jax.ShapeDtypeStruct((X_SIZE, types, rows), f32),
            jax.ShapeDtypeStruct((X_SIZE, STAT_ROWS, X_SIZE * rows), f32),
        ],
        scratch_shapes=[pltpu.VMEM((types, rows), f32)],
        compiler_params=params(),
        name="scores",
    )(logit_scale, place, gathered, table)
    stats = lax.all_to_all(stats, "gx", 0, 0, tiled=True)
    grads, type_part, scale_part = pl.pallas_call(
        grads_kernel,
        grid=(X_SIZE,),
        in_specs=[
            smem,
            smem,
            tile(types, rows),
            pl.BlockSpec((X_SIZE, STAT_ROWS, rows), lambda j: (0, 0, j)),
            tile(sent_rows, width),
        ],
        out_specs=[tile(types, rows), whole(types, width), whole(1, 128)],
        out_shape=[
            jax.ShapeDtypeStruct((X_SIZE, types, rows), bf16),
            jax.ShapeDtypeStruct((types, width), bf16),
            jax.ShapeDtypeStruct((1, 128), f32),
        ],
        scratch_shapes=[pltpu.VMEM((types, width), f32), pltpu.VMEM((1, rows), f32)],
        compiler_params=params(),
        name="grads",
    )(logit_scale, place, exps, stats, gathered)
    type_grad = lax.psum_scatter(type_part, "gz", scatter_dimension=0, tiled=True)
    mention_part, scale_parts = pl.pallas_call(
        mention_kernel,
        grid=(X_SIZE,),
        in_specs=[smem, whole(1, 128), tile(types, rows), whole(types, width)],
        out_specs=[tile(rows, width), whole(Z_SIZE * cols, 1, 128)],
        out_shape=[
            jax.ShapeDtypeStruct((X_SIZE, rows, width), bf16),
            jax.ShapeDtypeStruct((Z_SIZE * cols, 1, 128), f32),
        ],
        compiler_params=params(),
        name="mention_part",
    )(logit_scale, scale_part, grads, table)
    mention_grad = lax.all_to_all(mention_part, "gx", 0, 0, tiled=True)
    mention_grad = jnp.sum(mention_grad, axis=0, dtype=f32).astype(bf16)
    scale_parts = lax.all_to_all(scale_parts, ("gz", "gy"), 0, 0, tiled=True)
    scale_grad = (jnp.sum(scale_parts[:, 0, 0]) / (rows * devices)).reshape(1)
    new_table, new_first, new_second = adam_rows(
        type_table, adam_m, adam_v, type_grad.astype(f32)
    )
    return (new_table, new_first, new_second, mention_grad, scale_grad)


def solution(mesh):
    gx, gy = mesh.devices.shape
    split = Mesh(mesh.devices.reshape(gx // X_SIZE, X_SIZE, gy), ("gz", "gx", "gy"))
    axes = ("gz", "gx", "gy")
    rows = P(axes, None)
    return jax.shard_map(
        per_device,
        mesh=split,
        in_specs=(rows, rows, rows, rows, P(), rows, P(axes), P(axes), P(axes)),
        out_specs=(rows, rows, rows, rows, P()),
        check_vma=False,
    )
```

```python
import jax
import jax.numpy as jnp
from jax import lax
from jax.experimental import pallas as pl
from jax.experimental.pallas import tpu as pltpu
from jax.sharding import Mesh, PartitionSpec as P

beta_one = 0.9
beta_two = 0.999
learn_rate = 0.02
adam_eps = 1e-08
first_fix = 0.9999734386011124
second_fix = 0.09520785288629038

X_SIZE = 4
Z_SIZE = 8
BLOCK = 128
LOW = -1e30
META_ROWS = 32
SLOTS = 16
STAT_ROWS = 8
f32 = jnp.float32
bf16 = jnp.bfloat16


def cast_kernel(t_ref, out_ref):
    block = t_ref[...].astype(bf16)
    for k in range(out_ref.shape[0]):
        out_ref[k] = block


def pack_kernel(
    cols, list_hbm, len_hbm, slot_hbm, row_hbm, m_hbm, out_ref, list_ref, len_ref, slot_ref, row_ref, sems
):
    rows, width = m_hbm.shape
    pairs = [(list_hbm, list_ref), (len_hbm, len_ref), (slot_hbm, slot_ref), (row_hbm, row_ref)]
    pairs.append((m_hbm, out_ref.at[pl.ds(0, rows), :]))
    copies = [pltpu.make_async_copy(src, dst, sems.at[i]) for i, (src, dst) in enumerate(pairs)]
    for copy in copies:
        copy.start()
    for copy in copies[:4]:
        copy.wait()
    owners = lax.div(list_ref[...], cols).astype(f32)
    lens = len_ref[...]
    first = lax.broadcasted_iota(jnp.int32, (1, rows), 1) < BLOCK
    length = jnp.where(first, lens[:, 0:1], lens[:, 1:2])
    slot = slot_ref[...]
    gold = jnp.zeros((1, rows), f32)
    lines = []
    for k in range(SLOTS):
        owner = jnp.where(first, owners[0:1, k : k + 1], owners[1:2, k : k + 1])
        gold = gold + jnp.where(slot == k, owner, 0.0)
        lines.append(jnp.where(length > k, owner, -1.0))
    lines += [gold, row_ref[...].astype(f32)]
    lines.append(jnp.zeros((META_ROWS - len(lines), rows), f32))
    out_ref[rows : rows + META_ROWS, :] = jnp.zeros((META_ROWS, width), bf16)
    out_ref[rows : rows + META_ROWS, 0:rows] = jnp.concatenate(lines, axis=0).astype(bf16)
    copies[4].wait()


def owner_at(place_ref, line):
    return (line * X_SIZE + place_ref[1]).astype(f32)


def tile_from(place_ref, step):
    return lax.rem(place_ref[1] - step + X_SIZE, X_SIZE)


def join_types(place_ref, near_ref, below_ref, above_ref, tile_ref):
    parity = lax.rem(place_ref[0], 2)
    half = Z_SIZE // 4
    for k in range(Z_SIZE // 2):
        other = below_ref[k] if k < half else above_ref[k - half]
        tile_ref[pl.ds(pl.multiple_of((2 * k + parity) * BLOCK, BLOCK), BLOCK), :] = near_ref[k]
        tile_ref[pl.ds(pl.multiple_of((2 * k + 1 - parity) * BLOCK, BLOCK), BLOCK), :] = other


def scores_kernel(
    factor_ref, place_ref, m_ref, near_ref, below_ref, above_ref, exp_ref, stat_ref, tile_ref, raw_ref
):
    step = pl.program_id(0)
    factor = factor_ref[0]
    rows = m_ref.shape[1] - META_ROWS

    @pl.when(step == 0)
    def _():
        join_types(place_ref, near_ref, below_ref, above_ref, tile_ref)

    raw_ref[...] = lax.dot_general(
        tile_ref[...], m_ref[0, 0:rows, :], (((1,), (1,)), ((), ())), preferred_element_type=f32
    )
    meta = m_ref[0, rows : rows + META_ROWS, 0:rows].astype(f32)
    owners = meta[0:SLOTS, :]
    gold_owner = meta[SLOTS : SLOTS + 1, :]
    gold_row = meta[SLOTS + 1 : SLOTS + 2, :].astype(jnp.int32)
    ids = lax.broadcasted_iota(jnp.int32, (BLOCK, rows), 0)
    top = jnp.full((1, rows), LOW, f32)
    gold_raw = jnp.zeros((1, rows), f32)
    lives = []
    for c in range(Z_SIZE):
        owner = owner_at(place_ref, c)
        lives.append(jnp.max(jnp.where(owners == owner, 1.0, 0.0), axis=0, keepdims=True) > 0.0)
        raw = raw_ref[c * BLOCK : (c + 1) * BLOCK, :]
        top = jnp.maximum(top, jnp.where(lives[c], jnp.max(raw, axis=0, keepdims=True), LOW))
        gold = jnp.where(gold_owner == owner, gold_row, -1)
        gold_raw = gold_raw + jnp.sum(jnp.where(ids == gold, raw, 0.0), axis=0, keepdims=True)
    total = jnp.zeros((1, rows), f32)
    mass = jnp.zeros((1, rows), f32)
    for c in range(Z_SIZE):
        below = jnp.where(lives[c], top, -LOW)
        gap = raw_ref[c * BLOCK : (c + 1) * BLOCK, :] - below
        weights = jnp.exp(factor * gap)
        exp_ref[0, c * BLOCK : (c + 1) * BLOCK, :] = weights
        total = total + jnp.sum(weights, axis=0, keepdims=True)
        mass = mass + jnp.sum(weights * gap, axis=0, keepdims=True)
    stat = jnp.concatenate(
        [top, total, mass, gold_raw, jnp.zeros((STAT_ROWS - 4, rows), f32)], axis=0
    )
    at = pl.multiple_of(tile_from(place_ref, step) * rows, BLOCK)
    for d in range(stat_ref.shape[0]):
        stat_ref[d, :, pl.ds(at, rows)] = stat


def merge_stats(factor, place_ref, stat_ref, share_ref, scale_ref):
    tops = stat_ref[:, 0, :]
    sums = stat_ref[:, 1, :]
    top = jnp.max(tops, axis=0, keepdims=True)
    shares = jnp.exp(factor * (tops - top))
    total = jnp.sum(sums * shares, axis=0, keepdims=True)
    masses = stat_ref[:, 2, :] + sums * tops
    mass = jnp.sum(jnp.where(sums > 0.0, masses * shares, 0.0), axis=0, keepdims=True)
    scale = mass / total - jnp.sum(stat_ref[:, 3, :], axis=0, keepdims=True)
    scale_ref[...] = jnp.broadcast_to(jnp.sum(scale, axis=1, keepdims=True), scale_ref.shape)
    ids = lax.broadcasted_iota(jnp.int32, tops.shape, 0)
    own = jnp.max(jnp.where(ids == place_ref[1], tops, LOW), axis=0, keepdims=True)
    share_ref[...] = jnp.exp(factor * (own - top) - jnp.log(total))


def grads_kernel(
    factor_ref, place_ref, exp_ref, stat_ref, m_ref, g_ref, type_ref, scale_ref, share_ref, rows_ref, grad_ref
):
    step = pl.program_id(0)
    factor = factor_ref[0]
    rows = m_ref.shape[1] - META_ROWS
    chunk = exp_ref.shape[1]

    @pl.when(step == 0)
    def _():
        merge_stats(factor, place_ref, stat_ref, share_ref, scale_ref)
        for s in range(X_SIZE):
            rows_ref[s * rows : (s + 1) * rows, :] = m_ref[s, 0:rows, :]

    ids = lax.broadcasted_iota(jnp.int32, (BLOCK, rows), 0)
    for s in range(X_SIZE):
        at = pl.multiple_of(tile_from(place_ref, s) * rows, BLOCK)
        share = share_ref[:, pl.ds(at, rows)]
        gold_owner = m_ref[s, rows + SLOTS : rows + META_ROWS, 0:rows].astype(f32)[0:1, :]
        gold_row = m_ref[s, rows + SLOTS : rows + META_ROWS, 0:rows].astype(f32)[1:2, :]
        for c in range(chunk // BLOCK):
            owner = owner_at(place_ref, step * (chunk // BLOCK) + c)
            gold = jnp.where(gold_owner == owner, gold_row, -1.0).astype(jnp.int32)
            weights = share * exp_ref[s, c * BLOCK : (c + 1) * BLOCK, :]
            grad = (weights - jnp.where(ids == gold, 1.0, 0.0)).astype(bf16)
            g_ref[s, c * BLOCK : (c + 1) * BLOCK, :] = grad
            grad_ref[c * BLOCK : (c + 1) * BLOCK, s * rows : (s + 1) * rows] = grad
    part = jnp.dot(grad_ref[...], rows_ref[...], preferred_element_type=f32)
    type_ref[...] = (factor * part).astype(bf16)


def mention_kernel(
    factor_ref, place_ref, scale_ref, g_ref, near_ref, below_ref, above_ref, *refs
):
    out_refs, (scales_ref, tile_ref) = refs[:X_SIZE], refs[X_SIZE:]
    step = pl.program_id(0)

    @pl.when(step == 0)
    def _():
        join_types(place_ref, near_ref, below_ref, above_ref, tile_ref)
        scales_ref[...] = jnp.broadcast_to(scale_ref[...][None], scales_ref.shape)

    part = lax.dot_general(
        g_ref[0], tile_ref[...], (((0,), (0,)), ((), ())), preferred_element_type=f32
    )
    part = (factor_ref[0] * part).astype(bf16)
    for s, out_ref in enumerate(out_refs):

        @pl.when(step == s)
        def _(out_ref=out_ref):
            out_ref[...] = part


def adam_rows(type_table, adam_m, adam_v, type_grad):
    moment_one = beta_one * adam_m + (1.0 - beta_one) * type_grad
    moment_two = beta_two * adam_v + (1.0 - beta_two) * type_grad * type_grad
    updated = type_table - learn_rate * (moment_one / first_fix) / (
        jnp.sqrt(moment_two / second_fix) + adam_eps
    )
    return (updated, moment_one, moment_two)


def params(mib=60):
    return pltpu.CompilerParams(vmem_limit_bytes=mib * 1024 * 1024)


def shifted(array, axis, by):
    size = lax.axis_size(axis)
    return lax.ppermute(array, axis, [(i, (i + by) % size) for i in range(size)])


def per_device(
    mentions,
    type_table,
    adam_m,
    adam_v,
    logit_scale,
    block_lists,
    list_lengths,
    gold_slot,
    gold_row,
):
    cols = lax.axis_size("gy")
    devices = Z_SIZE * X_SIZE * cols
    block_rows, width = type_table.shape
    rows = mentions.shape[0]
    sent_rows = rows + META_ROWS
    types = Z_SIZE * block_rows
    smem = pl.BlockSpec(memory_space=pltpu.SMEM)
    hbm = pl.BlockSpec(memory_space=pltpu.HBM)
    place = jnp.stack([lax.axis_index("gz"), lax.axis_index("gx")]).astype(jnp.int32)
    half = Z_SIZE // 2

    def tile(*shape):
        return pl.BlockSpec((1,) + shape, lambda j: (j, 0, 0))

    def whole(*shape):
        return pl.BlockSpec(shape, lambda j: (0,) * len(shape))

    copies = pl.pallas_call(
        cast_kernel,
        out_shape=jax.ShapeDtypeStruct((half, block_rows, width), bf16),
        compiler_params=params(),
        name="cast",
    )(type_table)
    parities = [list(range(p, Z_SIZE, 2)) for p in range(2)]
    near = lax.all_to_all(copies, "gz", 0, 0, tiled=True, axis_index_groups=parities)
    lower = shifted(near[: half // 2], "gz", 1)
    upper = shifted(near[half // 2 :], "gz", -1)
    table = (near, lower, upper)
    table_specs = [whole(t.shape[0], block_rows, width) for t in table]
    packed = pl.pallas_call(
        lambda *refs: pack_kernel(cols, *refs),
        in_specs=[hbm] * 5,
        out_shape=jax.ShapeDtypeStruct((sent_rows, width), bf16),
        scratch_shapes=[
            pltpu.VMEM((2, SLOTS), jnp.int32),
            pltpu.VMEM((1, 2), jnp.int32),
            pltpu.VMEM((1, rows), jnp.int32),
            pltpu.VMEM((1, rows), jnp.int32),
            pltpu.SemaphoreType.DMA((5,)),
        ],
        compiler_params=params(),
        name="pack",
    )(
        block_lists,
        list_lengths.reshape(1, 2),
        gold_slot.reshape(1, rows),
        gold_row.reshape(1, rows),
        mentions,
    )
    gathered = jnp.stack([packed] + [shifted(packed, "gx", s) for s in range(1, X_SIZE)])

    exps, stats = pl.pallas_call(
        scores_kernel,
        grid=(X_SIZE,),
        in_specs=[smem, smem, tile(sent_rows, width)] + table_specs,
        out_specs=[tile(types, rows), whole(X_SIZE, STAT_ROWS, X_SIZE * rows)],
        out_shape=[
            jax.ShapeDtypeStruct((X_SIZE, types, rows), f32),
            jax.ShapeDtypeStruct((X_SIZE, STAT_ROWS, X_SIZE * rows), f32),
        ],
        scratch_shapes=[pltpu.VMEM((types, width), bf16), pltpu.VMEM((types, rows), f32)],
        compiler_params=params(50),
        name="scores",
    )(logit_scale, place, gathered, *table)
    stats = lax.all_to_all(stats, "gx", 0, 0, tiled=True)
    chunk = 2 * block_rows
    chunk_spec = pl.BlockSpec((X_SIZE, chunk, rows), lambda i: (0, i, 0))
    grads, type_part, scale_part = pl.pallas_call(
        grads_kernel,
        grid=(types // chunk,),
        in_specs=[
            smem,
            smem,
            chunk_spec,
            whole(X_SIZE, STAT_ROWS, X_SIZE * rows),
            whole(X_SIZE, sent_rows, width),
        ],
        out_specs=[chunk_spec, pl.BlockSpec((chunk, width), lambda i: (i, 0)), whole(1, 128)],
        out_shape=[
            jax.ShapeDtypeStruct((X_SIZE, types, rows), bf16),
            jax.ShapeDtypeStruct((types, width), bf16),
            jax.ShapeDtypeStruct((1, 128), f32),
        ],
        scratch_shapes=[
            pltpu.VMEM((1, X_SIZE * rows), f32),
            pltpu.VMEM((X_SIZE * rows, width), bf16),
            pltpu.VMEM((chunk, X_SIZE * rows), bf16),
        ],
        compiler_params=params(50),
        name="grads",
    )(logit_scale, place, exps, stats, gathered)
    type_grad = lax.psum_scatter(type_part, "gz", scatter_dimension=0, tiled=True)
    *parts, scale_parts = pl.pallas_call(
        mention_kernel,
        grid=(X_SIZE,),
        in_specs=[smem, smem, whole(1, 128), tile(types, rows)] + table_specs,
        out_specs=[whole(rows, width)] * X_SIZE + [whole(Z_SIZE * cols, 1, 128)],
        out_shape=[jax.ShapeDtypeStruct((rows, width), bf16)] * X_SIZE
        + [jax.ShapeDtypeStruct((Z_SIZE * cols, 1, 128), f32)],
        scratch_shapes=[pltpu.VMEM((types, width), bf16)],
        compiler_params=params(50),
        name="mention_part",
    )(logit_scale, place, scale_part, grads, *table)
    mention_grad = parts[0].astype(f32)
    for s in range(1, X_SIZE):
        mention_grad = mention_grad + shifted(parts[s], "gx", -s).astype(f32)
    mention_grad = mention_grad.astype(bf16)
    scale_parts = lax.all_to_all(scale_parts, ("gz", "gy"), 0, 0, tiled=True)
    scale_grad = (jnp.sum(scale_parts[:, 0, 0]) / (rows * devices)).reshape(1)
    new_table, new_first, new_second = adam_rows(
        type_table, adam_m, adam_v, type_grad.astype(f32)
    )
    return (new_table, new_first, new_second, mention_grad, scale_grad)


def solution(mesh):
    gx, gy = mesh.devices.shape
    split = Mesh(mesh.devices.reshape(gx // X_SIZE, X_SIZE, gy), ("gz", "gx", "gy"))
    axes = ("gz", "gx", "gy")
    rows = P(axes, None)
    return jax.shard_map(
        per_device,
        mesh=split,
        in_specs=(rows, rows, rows, rows, P(), rows, P(axes), P(axes), P(axes)),
        out_specs=(rows, rows, rows, rows, P()),
        check_vma=False,
    )
```

```python
import jax
import jax.numpy as jnp
from jax import lax
from jax.experimental import pallas as pl
from jax.experimental.pallas import tpu as pltpu
from jax.sharding import Mesh, PartitionSpec as P

beta_one = 0.9
beta_two = 0.999
learn_rate = 0.02
adam_eps = 1e-08
first_fix = 0.9999734386011124
second_fix = 0.09520785288629038

X_SIZE = 4
Z_SIZE = 8
BLOCK = 128
LOW = -1e30
META_ROWS = 32
SLOTS = 16
STAT_ROWS = 8
f32 = jnp.float32
bf16 = jnp.bfloat16


def cast_kernel(t_ref, out_ref):
    block = t_ref[...].astype(bf16)
    for k in range(out_ref.shape[0]):
        out_ref[k] = block


def pack_kernel(
    cols, list_hbm, len_hbm, slot_hbm, row_hbm, m_hbm, out_ref, list_ref, len_ref, slot_ref, row_ref, sems
):
    rows, width = m_hbm.shape
    pairs = [(list_hbm, list_ref), (len_hbm, len_ref), (slot_hbm, slot_ref), (row_hbm, row_ref)]
    pairs.append((m_hbm, out_ref.at[pl.ds(0, rows), :]))
    copies = [pltpu.make_async_copy(src, dst, sems.at[i]) for i, (src, dst) in enumerate(pairs)]
    for copy in copies:
        copy.start()
    for copy in copies[:4]:
        copy.wait()
    owners = lax.div(list_ref[...], cols).astype(f32)
    lens = len_ref[...]
    first = lax.broadcasted_iota(jnp.int32, (1, rows), 1) < BLOCK
    length = jnp.where(first, lens[:, 0:1], lens[:, 1:2])
    slot = slot_ref[...]
    gold = jnp.zeros((1, rows), f32)
    lines = []
    for k in range(SLOTS):
        owner = jnp.where(first, owners[0:1, k : k + 1], owners[1:2, k : k + 1])
        gold = gold + jnp.where(slot == k, owner, 0.0)
        lines.append(jnp.where(length > k, owner, -1.0))
    lines += [gold, row_ref[...].astype(f32)]
    lines.append(jnp.zeros((META_ROWS - len(lines), rows), f32))
    out_ref[rows : rows + META_ROWS, :] = jnp.zeros((META_ROWS, width), bf16)
    out_ref[rows : rows + META_ROWS, 0:rows] = jnp.concatenate(lines, axis=0).astype(bf16)
    copies[4].wait()


def owner_at(place_ref, line):
    return (line * X_SIZE + place_ref[1]).astype(f32)


def tile_from(place_ref, step):
    return jnp.bitwise_xor(place_ref[1], step)


def join_types(place_ref, near_ref, low_ref, high_ref, tile_ref):
    parity = lax.rem(place_ref[0], 2)
    half = Z_SIZE // 4
    for k in range(Z_SIZE // 2):
        other = low_ref[k] if k < half else high_ref[k - half]
        tile_ref[pl.ds(pl.multiple_of((2 * k + parity) * BLOCK, BLOCK), BLOCK), :] = near_ref[k]
        tile_ref[pl.ds(pl.multiple_of((2 * k + 1 - parity) * BLOCK, BLOCK), BLOCK), :] = other


def score_half(factor, place_ref, shift, m_ref, tile_ref, raw_ref, exp_ref):
    rows = m_ref.shape[1] - META_ROWS
    raw_ref[...] = lax.dot_general(
        tile_ref[...], m_ref[0, 0:rows, :], (((1,), (1,)), ((), ())), preferred_element_type=f32
    )
    meta = m_ref[0, rows : rows + META_ROWS, 0:rows].astype(f32)
    owners = meta[0:SLOTS, :]
    gold_owner = meta[SLOTS : SLOTS + 1, :]
    gold_row = meta[SLOTS + 1 : SLOTS + 2, :].astype(jnp.int32)
    ids = lax.broadcasted_iota(jnp.int32, (BLOCK, rows), 0)
    top = jnp.full((1, rows), LOW, f32)
    gold_raw = jnp.zeros((1, rows), f32)
    lives = []
    for k in range(Z_SIZE // 2):
        owner = owner_at(place_ref, 2 * k + shift)
        lives.append(jnp.max(jnp.where(owners == owner, 1.0, 0.0), axis=0, keepdims=True) > 0.0)
        raw = raw_ref[k * BLOCK : (k + 1) * BLOCK, :]
        top = jnp.maximum(top, jnp.where(lives[k], jnp.max(raw, axis=0, keepdims=True), LOW))
        gold = jnp.where(gold_owner == owner, gold_row, -1)
        gold_raw = gold_raw + jnp.sum(jnp.where(ids == gold, raw, 0.0), axis=0, keepdims=True)
    total = jnp.zeros((1, rows), f32)
    mass = jnp.zeros((1, rows), f32)
    for k in range(Z_SIZE // 2):
        below = jnp.where(lives[k], top, -LOW)
        gap = raw_ref[k * BLOCK : (k + 1) * BLOCK, :] - below
        weights = jnp.exp(factor * gap)
        exp_ref[0, k * BLOCK : (k + 1) * BLOCK, :] = weights
        total = total + jnp.sum(weights, axis=0, keepdims=True)
        mass = mass + jnp.sum(weights * gap, axis=0, keepdims=True)
    return top, total, mass, gold_raw


def near_kernel(factor_ref, place_ref, m_ref, near_ref, exp_ref, stat_ref, tile_ref, raw_ref):
    step = pl.program_id(0)

    @pl.when(step == 0)
    def _():
        for k in range(near_ref.shape[0]):
            tile_ref[k * BLOCK : (k + 1) * BLOCK, :] = near_ref[k]

    shift = lax.rem(place_ref[0], 2)
    stats = score_half(factor_ref[0], place_ref, shift, m_ref, tile_ref, raw_ref, exp_ref)
    rows = stats[0].shape[1]
    rest = jnp.zeros((STAT_ROWS - len(stats), rows), f32)
    stat_ref[0] = jnp.concatenate(list(stats) + [rest], axis=0)


def far_kernel(
    factor_ref, place_ref, m_ref, low_ref, high_ref, part_ref, exp_ref, stat_ref, tile_ref, raw_ref
):
    step = pl.program_id(0)

    @pl.when(step == 0)
    def _():
        half = low_ref.shape[0]
        for k in range(2 * half):
            other = low_ref[k] if k < half else high_ref[k - half]
            tile_ref[k * BLOCK : (k + 1) * BLOCK, :] = other

    shift = 1 - lax.rem(place_ref[0], 2)
    top, total, mass, gold_raw = score_half(
        factor_ref[0], place_ref, shift, m_ref, tile_ref, raw_ref, exp_ref
    )
    rows = top.shape[1]
    near = part_ref[0]
    lines = [near[0:3, :], top, total, mass, gold_raw + near[3:4, :]]
    lines.append(jnp.zeros((STAT_ROWS - 7, rows), f32))
    stat = jnp.concatenate(lines, axis=0)
    at = pl.multiple_of(tile_from(place_ref, step) * rows, BLOCK)
    for d in range(stat_ref.shape[0]):
        stat_ref[d, :, pl.ds(at, rows)] = stat


def merge_stats(factor, place_ref, stat_ref, share_ref, scale_ref):
    tops, sums, masses = [
        jnp.concatenate([stat_ref[:, r, :], stat_ref[:, r + 3, :]], axis=0) for r in range(3)
    ]
    top = jnp.max(tops, axis=0, keepdims=True)
    shares = jnp.exp(factor * (tops - top))
    total = jnp.sum(sums * shares, axis=0, keepdims=True)
    masses = masses + sums * tops
    mass = jnp.sum(jnp.where(sums > 0.0, masses * shares, 0.0), axis=0, keepdims=True)
    scale = mass / total - jnp.sum(stat_ref[:, 6, :], axis=0, keepdims=True)
    scale_ref[...] = jnp.broadcast_to(jnp.sum(scale, axis=1, keepdims=True), scale_ref.shape)
    ids = lax.broadcasted_iota(jnp.int32, tops.shape, 0)
    for h in range(2):
        mine = ids == place_ref[1] + h * X_SIZE
        own = jnp.max(jnp.where(mine, tops, LOW), axis=0, keepdims=True)
        share_ref[h : h + 1, :] = jnp.exp(factor * (own - top) - jnp.log(total))


def grads_kernel(
    factor_ref, place_ref, near_ref, far_ref, stat_ref, m_ref, g_ref, type_ref, scale_ref, share_ref, rows_ref, grad_ref
):
    step = pl.program_id(0)
    factor = factor_ref[0]
    rows = m_ref.shape[1] - META_ROWS

    @pl.when(step == 0)
    def _():
        merge_stats(factor, place_ref, stat_ref, share_ref, scale_ref)
        for s in range(X_SIZE):
            rows_ref[s * rows : (s + 1) * rows, :] = m_ref[s, 0:rows, :]

    ids = lax.broadcasted_iota(jnp.int32, (BLOCK, rows), 0)
    parity = lax.rem(place_ref[0], 2)
    for s in range(X_SIZE):
        at = pl.multiple_of(tile_from(place_ref, s) * rows, BLOCK)
        meta = m_ref[s, rows + SLOTS : rows + META_ROWS, 0:rows].astype(f32)
        gold_owner = meta[0:1, :]
        gold_row = meta[1:2, :]
        for h, exp_ref in enumerate((near_ref, far_ref)):
            place = parity if h == 0 else 1 - parity
            owner = owner_at(place_ref, 2 * step + place)
            gold = jnp.where(gold_owner == owner, gold_row, -1.0).astype(jnp.int32)
            weights = share_ref[h : h + 1, pl.ds(at, rows)] * exp_ref[s]
            grad = (weights - jnp.where(ids == gold, 1.0, 0.0)).astype(bf16)
            line = pl.ds(pl.multiple_of(place * BLOCK, BLOCK), BLOCK)
            g_ref[s, line, :] = grad
            grad_ref[line, s * rows : (s + 1) * rows] = grad
    part = jnp.dot(grad_ref[...], rows_ref[...], preferred_element_type=f32)
    type_ref[...] = (factor * part).astype(bf16)


def mention_kernel(
    factor_ref, place_ref, scale_ref, g_ref, near_ref, low_ref, high_ref, *refs
):
    out_refs, (scales_ref, tile_ref) = refs[:X_SIZE], refs[X_SIZE:]
    step = pl.program_id(0)

    @pl.when(step == 0)
    def _():
        join_types(place_ref, near_ref, low_ref, high_ref, tile_ref)
        scales_ref[...] = jnp.broadcast_to(scale_ref[...][None], scales_ref.shape)

    part = lax.dot_general(
        g_ref[0], tile_ref[...], (((0,), (0,)), ((), ())), preferred_element_type=f32
    )
    part = (factor_ref[0] * part).astype(bf16)
    for s, out_ref in enumerate(out_refs):

        @pl.when(step == s)
        def _(out_ref=out_ref):
            out_ref[...] = part


def adam_rows(type_table, adam_m, adam_v, type_grad):
    moment_one = beta_one * adam_m + (1.0 - beta_one) * type_grad
    moment_two = beta_two * adam_v + (1.0 - beta_two) * type_grad * type_grad
    updated = type_table - learn_rate * (moment_one / first_fix) / (
        jnp.sqrt(moment_two / second_fix) + adam_eps
    )
    return (updated, moment_one, moment_two)


def params(mib=60):
    return pltpu.CompilerParams(vmem_limit_bytes=mib * 1024 * 1024)


def paired(array, axis, partner):
    return lax.ppermute(array, axis, [(i, partner(i)) for i in range(lax.axis_size(axis))])


def per_device(
    mentions,
    type_table,
    adam_m,
    adam_v,
    logit_scale,
    block_lists,
    list_lengths,
    gold_slot,
    gold_row,
):
    cols = lax.axis_size("gy")
    devices = Z_SIZE * X_SIZE * cols
    block_rows, width = type_table.shape
    rows = mentions.shape[0]
    sent_rows = rows + META_ROWS
    types = Z_SIZE * block_rows
    smem = pl.BlockSpec(memory_space=pltpu.SMEM)
    hbm = pl.BlockSpec(memory_space=pltpu.HBM)
    place = jnp.stack([lax.axis_index("gz"), lax.axis_index("gx")]).astype(jnp.int32)
    half = Z_SIZE // 2

    def tile(*shape):
        return pl.BlockSpec((1,) + shape, lambda j: (j, 0, 0))

    def whole(*shape):
        return pl.BlockSpec(shape, lambda j: (0,) * len(shape))

    copies = pl.pallas_call(
        cast_kernel,
        out_shape=jax.ShapeDtypeStruct((half, block_rows, width), bf16),
        compiler_params=params(),
        name="cast",
    )(type_table)
    parities = [list(range(p, Z_SIZE, 2)) for p in range(2)]
    near = lax.all_to_all(copies, "gz", 0, 0, tiled=True, axis_index_groups=parities)
    low = paired(near[: half // 2], "gz", lambda z: z ^ 1)
    high = paired(near[half // 2 :], "gz", lambda z: ((z + 1) ^ 1) - 1 & Z_SIZE - 1)
    table = (near, low, high)
    table_specs = [whole(t.shape[0], block_rows, width) for t in table]
    packed = pl.pallas_call(
        lambda *refs: pack_kernel(cols, *refs),
        in_specs=[hbm] * 5,
        out_shape=jax.ShapeDtypeStruct((sent_rows, width), bf16),
        scratch_shapes=[
            pltpu.VMEM((2, SLOTS), jnp.int32),
            pltpu.VMEM((1, 2), jnp.int32),
            pltpu.VMEM((1, rows), jnp.int32),
            pltpu.VMEM((1, rows), jnp.int32),
            pltpu.SemaphoreType.DMA((5,)),
        ],
        compiler_params=params(),
        name="pack",
    )(
        block_lists,
        list_lengths.reshape(1, 2),
        gold_slot.reshape(1, rows),
        gold_row.reshape(1, rows),
        mentions,
    )
    gathered = jnp.stack(
        [packed] + [paired(packed, "gx", lambda x, s=s: x ^ s) for s in range(1, X_SIZE)]
    )

    half_types = half * block_rows
    scratch = [pltpu.VMEM((half_types, width), bf16), pltpu.VMEM((half_types, rows), f32)]
    exps_shape = jax.ShapeDtypeStruct((X_SIZE, half_types, rows), f32)
    near_exps, near_stats = pl.pallas_call(
        near_kernel,
        grid=(X_SIZE,),
        in_specs=[smem, smem, tile(sent_rows, width)] + table_specs[:1],
        out_specs=[tile(half_types, rows), tile(STAT_ROWS, rows)],
        out_shape=[exps_shape, jax.ShapeDtypeStruct((X_SIZE, STAT_ROWS, rows), f32)],
        scratch_shapes=scratch,
        compiler_params=params(16),
        name="near_scores",
    )(logit_scale, place, gathered, near)
    far_exps, stats = pl.pallas_call(
        far_kernel,
        grid=(X_SIZE,),
        in_specs=[smem, smem, tile(sent_rows, width)] + table_specs[1:] + [tile(STAT_ROWS, rows)],
        out_specs=[tile(half_types, rows), whole(X_SIZE, STAT_ROWS, X_SIZE * rows)],
        out_shape=[exps_shape, jax.ShapeDtypeStruct((X_SIZE, STAT_ROWS, X_SIZE * rows), f32)],
        scratch_shapes=scratch,
        compiler_params=params(16),
        name="far_scores",
    )(logit_scale, place, gathered, low, high, near_stats)
    stats = lax.all_to_all(stats, "gx", 0, 0, tiled=True)
    chunk = 2 * block_rows
    chunk_spec = pl.BlockSpec((X_SIZE, chunk, rows), lambda i: (0, i, 0))
    grads, type_part, scale_part = pl.pallas_call(
        grads_kernel,
        grid=(types // chunk,),
        in_specs=[
            smem,
            smem,
            pl.BlockSpec((X_SIZE, block_rows, rows), lambda i: (0, i, 0)),
            pl.BlockSpec((X_SIZE, block_rows, rows), lambda i: (0, i, 0)),
            whole(X_SIZE, STAT_ROWS, X_SIZE * rows),
            whole(X_SIZE, sent_rows, width),
        ],
        out_specs=[chunk_spec, pl.BlockSpec((chunk, width), lambda i: (i, 0)), whole(1, 128)],
        out_shape=[
            jax.ShapeDtypeStruct((X_SIZE, types, rows), bf16),
            jax.ShapeDtypeStruct((types, width), bf16),
            jax.ShapeDtypeStruct((1, 128), f32),
        ],
        scratch_shapes=[
            pltpu.VMEM((2, X_SIZE * rows), f32),
            pltpu.VMEM((X_SIZE * rows, width), bf16),
            pltpu.VMEM((chunk, X_SIZE * rows), bf16),
        ],
        compiler_params=params(16),
        name="grads",
    )(logit_scale, place, near_exps, far_exps, stats, gathered)
    type_grad = lax.psum_scatter(type_part, "gz", scatter_dimension=0, tiled=True)
    *parts, scale_parts = pl.pallas_call(
        mention_kernel,
        grid=(X_SIZE,),
        in_specs=[smem, smem, whole(1, 128), tile(types, rows)] + table_specs,
        out_specs=[whole(rows, width)] * X_SIZE + [whole(Z_SIZE * cols, 1, 128)],
        out_shape=[jax.ShapeDtypeStruct((rows, width), bf16)] * X_SIZE
        + [jax.ShapeDtypeStruct((Z_SIZE * cols, 1, 128), f32)],
        scratch_shapes=[pltpu.VMEM((types, width), bf16)],
        compiler_params=params(16),
        name="mention_part",
    )(logit_scale, place, scale_part, grads, *table)
    mention_grad = parts[0].astype(f32)
    for s in range(1, X_SIZE):
        mention_grad = mention_grad + paired(
            parts[s], "gx", lambda x, s=s: x ^ s
        ).astype(f32)
    mention_grad = mention_grad.astype(bf16)
    scale_parts = lax.all_to_all(scale_parts, ("gz", "gy"), 0, 0, tiled=True)
    scale_grad = (jnp.sum(scale_parts[:, 0, 0]) / (rows * devices)).reshape(1)
    new_table, new_first, new_second = adam_rows(
        type_table, adam_m, adam_v, type_grad.astype(f32)
    )
    return (new_table, new_first, new_second, mention_grad, scale_grad)


def solution(mesh):
    gx, gy = mesh.devices.shape
    split = Mesh(mesh.devices.reshape(gx // X_SIZE, X_SIZE, gy), ("gz", "gx", "gy"))
    axes = ("gz", "gx", "gy")
    rows = P(axes, None)
    return jax.shard_map(
        per_device,
        mesh=split,
        in_specs=(rows, rows, rows, rows, P(), rows, P(axes), P(axes), P(axes)),
        out_specs=(rows, rows, rows, rows, P()),
        check_vma=False,
    )
```

```python
import jax
import jax.numpy as jnp
from jax import lax
from jax.experimental import pallas as pl
from jax.experimental.pallas import tpu as pltpu
from jax.sharding import Mesh, PartitionSpec as P

beta_one = 0.9
beta_two = 0.999
learn_rate = 0.02
adam_eps = 1e-08
first_fix = 0.9999734386011124
second_fix = 0.09520785288629038

X_SIZE = 4
Z_SIZE = 8
BLOCK = 128
LOW = -1e30
META_ROWS = 32
SLOTS = 16
STAT_ROWS = 8
f32 = jnp.float32
bf16 = jnp.bfloat16


def cast_kernel(t_ref, own_ref, out_ref):
    block = t_ref[...].astype(bf16)
    own_ref[...] = block
    for k in range(out_ref.shape[0]):
        out_ref[k] = block


def pack_kernel(
    cols, list_hbm, len_hbm, slot_hbm, row_hbm, m_hbm, out_ref, list_ref, len_ref, slot_ref, row_ref, sems
):
    rows, width = m_hbm.shape
    pairs = [(list_hbm, list_ref), (len_hbm, len_ref), (slot_hbm, slot_ref), (row_hbm, row_ref)]
    pairs.append((m_hbm, out_ref.at[pl.ds(0, rows), :]))
    copies = [pltpu.make_async_copy(src, dst, sems.at[i]) for i, (src, dst) in enumerate(pairs)]
    for copy in copies:
        copy.start()
    for copy in copies[:4]:
        copy.wait()
    owners = lax.div(list_ref[...], cols).astype(f32)
    lens = len_ref[...]
    first = lax.broadcasted_iota(jnp.int32, (1, rows), 1) < BLOCK
    length = jnp.where(first, lens[:, 0:1], lens[:, 1:2])
    slot = slot_ref[...]
    gold = jnp.zeros((1, rows), f32)
    lines = []
    for k in range(SLOTS):
        owner = jnp.where(first, owners[0:1, k : k + 1], owners[1:2, k : k + 1])
        gold = gold + jnp.where(slot == k, owner, 0.0)
        lines.append(jnp.where(length > k, owner, -1.0))
    lines += [gold, row_ref[...].astype(f32)]
    lines.append(jnp.zeros((META_ROWS - len(lines), rows), f32))
    out_ref[rows : rows + META_ROWS, :] = jnp.zeros((META_ROWS, width), bf16)
    out_ref[rows : rows + META_ROWS, 0:rows] = jnp.concatenate(lines, axis=0).astype(bf16)
    copies[4].wait()


def owner_at(place_ref, line):
    return (line * X_SIZE + place_ref[1]).astype(f32)


def tile_from(place_ref, step):
    return jnp.bitwise_xor(place_ref[1], step)


def other_blocks(place):
    parity = lax.rem(place[0], 2)
    index = lax.div(place[0], 2)
    half = Z_SIZE // 2
    sign = 2 * parity - 1
    order = (index, index + sign + half, index - sign + half, index + half // 2)
    return parity, [lax.rem(k, half) for k in order]


def join_types(place_ref, near_ref, other_refs, tile_ref):
    parity, order = other_blocks(place_ref)
    lines = [2 * k + parity for k in range(Z_SIZE // 2)] + [2 * k + 1 - parity for k in order]
    blocks = [near_ref[k] for k in range(Z_SIZE // 2)] + [ref[...] for ref in other_refs]
    for line, block in zip(lines, blocks):
        tile_ref[pl.ds(pl.multiple_of(line * BLOCK, BLOCK), BLOCK), :] = block


def score_blocks(factor, place_ref, lines, m_ref, tile_ref, raw_ref, store):
    rows = m_ref.shape[1] - META_ROWS
    raw_ref[...] = lax.dot_general(
        tile_ref[...], m_ref[0, 0:rows, :], (((1,), (1,)), ((), ())), preferred_element_type=f32
    )
    meta = m_ref[0, rows : rows + META_ROWS, 0:rows].astype(f32)
    owners = meta[0:SLOTS, :]
    gold_owner = meta[SLOTS : SLOTS + 1, :]
    gold_row = meta[SLOTS + 1 : SLOTS + 2, :].astype(jnp.int32)
    ids = lax.broadcasted_iota(jnp.int32, (BLOCK, rows), 0)
    top = jnp.full((1, rows), LOW, f32)
    gold_raw = jnp.zeros((1, rows), f32)
    lives = []
    for k, line in enumerate(lines):
        owner = owner_at(place_ref, line)
        lives.append(jnp.max(jnp.where(owners == owner, 1.0, 0.0), axis=0, keepdims=True) > 0.0)
        raw = raw_ref[k * BLOCK : (k + 1) * BLOCK, :]
        top = jnp.maximum(top, jnp.where(lives[k], jnp.max(raw, axis=0, keepdims=True), LOW))
        gold = jnp.where(gold_owner == owner, gold_row, -1)
        gold_raw = gold_raw + jnp.sum(jnp.where(ids == gold, raw, 0.0), axis=0, keepdims=True)
    total = jnp.zeros((1, rows), f32)
    mass = jnp.zeros((1, rows), f32)
    for k in range(len(lines)):
        below = jnp.where(lives[k], top, -LOW)
        gap = raw_ref[k * BLOCK : (k + 1) * BLOCK, :] - below
        weights = jnp.exp(factor * gap)
        store(k, weights)
        total = total + jnp.sum(weights, axis=0, keepdims=True)
        mass = mass + jnp.sum(weights * gap, axis=0, keepdims=True)
    return top, total, mass, gold_raw


def near_kernel(
    factor_ref, place_ref, m_ref, near_ref, one_ref, two_ref, exp_ref, mid_ref, stat_ref, tile_ref, raw_ref
):
    half = Z_SIZE // 2

    @pl.when(pl.program_id(0) == 0)
    def _():
        for k in range(half):
            tile_ref[k * BLOCK : (k + 1) * BLOCK, :] = near_ref[k]
        for k, ref in enumerate((one_ref, two_ref)):
            tile_ref[(half + k) * BLOCK : (half + k + 1) * BLOCK, :] = ref[...]

    def store(k, weights):
        if k < half:
            exp_ref[0, k * BLOCK : (k + 1) * BLOCK, :] = weights
        else:
            mid_ref[0, (k - half) * BLOCK : (k - half + 1) * BLOCK, :] = weights

    parity, order = other_blocks(place_ref)
    lines = [2 * k + parity for k in range(half)] + [2 * k + 1 - parity for k in order[:2]]
    stats = score_blocks(factor_ref[0], place_ref, lines, m_ref, tile_ref, raw_ref, store)
    rows = stats[0].shape[1]
    rest = jnp.zeros((STAT_ROWS - len(stats), rows), f32)
    stat_ref[0] = jnp.concatenate(list(stats) + [rest], axis=0)


def far_kernel(
    factor_ref, place_ref, m_ref, low_ref, high_ref, mid_ref, part_ref, exp_ref, stat_ref, tile_ref, raw_ref
):
    step = pl.program_id(0)

    @pl.when(step == 0)
    def _():
        for k, ref in enumerate((low_ref, high_ref)):
            tile_ref[k * BLOCK : (k + 1) * BLOCK, :] = ref[...]

    parity, order = other_blocks(place_ref)

    def put(index, weights):
        exp_ref[0, pl.ds(pl.multiple_of(index * BLOCK, BLOCK), BLOCK), :] = weights

    for k in range(2):
        put(order[k], mid_ref[0, k * BLOCK : (k + 1) * BLOCK, :])
    lines = [2 * k + 1 - parity for k in order[2:]]
    top, total, mass, gold_raw = score_blocks(
        factor_ref[0],
        place_ref,
        lines,
        m_ref,
        tile_ref,
        raw_ref,
        lambda k, weights: put(order[2 + k], weights),
    )
    rows = top.shape[1]
    near = part_ref[0]
    lines = [near[0:3, :], top, total, mass, gold_raw + near[3:4, :]]
    lines.append(jnp.zeros((STAT_ROWS - 7, rows), f32))
    stat = jnp.concatenate(lines, axis=0)
    at = pl.multiple_of(tile_from(place_ref, step) * rows, BLOCK)
    for d in range(stat_ref.shape[0]):
        stat_ref[d, :, pl.ds(at, rows)] = stat


def merge_stats(factor, place_ref, stat_ref, share_ref, scale_ref):
    tops, sums, masses = [
        jnp.concatenate([stat_ref[:, r, :], stat_ref[:, r + 3, :]], axis=0) for r in range(3)
    ]
    top = jnp.max(tops, axis=0, keepdims=True)
    shares = jnp.exp(factor * (tops - top))
    total = jnp.sum(sums * shares, axis=0, keepdims=True)
    masses = masses + sums * tops
    mass = jnp.sum(jnp.where(sums > 0.0, masses * shares, 0.0), axis=0, keepdims=True)
    scale = mass / total - jnp.sum(stat_ref[:, 6, :], axis=0, keepdims=True)
    scale = jnp.sum(scale, axis=1, keepdims=True)
    scale_ref[...] = jnp.broadcast_to(scale[None], scale_ref.shape)
    ids = lax.broadcasted_iota(jnp.int32, tops.shape, 0)
    for h in range(2):
        mine = ids == place_ref[1] + h * X_SIZE
        own = jnp.max(jnp.where(mine, tops, LOW), axis=0, keepdims=True)
        share_ref[h : h + 1, :] = jnp.exp(factor * (own - top) - jnp.log(total))


def grads_kernel(
    factor_ref, place_ref, near_ref, far_ref, stat_ref, m_ref, g_ref, type_ref, scale_ref, share_ref, rows_ref, grad_ref
):
    step = pl.program_id(0)
    factor = factor_ref[0]
    rows = m_ref.shape[1] - META_ROWS

    @pl.when(step == 0)
    def _():
        merge_stats(factor, place_ref, stat_ref, share_ref, scale_ref)
        for s in range(X_SIZE):
            rows_ref[s * rows : (s + 1) * rows, :] = m_ref[s, 0:rows, :]

    ids = lax.broadcasted_iota(jnp.int32, (BLOCK, rows), 0)
    parity, order = other_blocks(place_ref)
    early = (step == order[0]) | (step == order[1])
    for s in range(X_SIZE):
        at = pl.multiple_of(tile_from(place_ref, s) * rows, BLOCK)
        meta = m_ref[s, rows + SLOTS : rows + META_ROWS, 0:rows].astype(f32)
        gold_owner = meta[0:1, :]
        gold_row = meta[1:2, :]
        for h, exp_ref in enumerate((near_ref, far_ref)):
            place = parity if h == 0 else 1 - parity
            owner = owner_at(place_ref, 2 * step + place)
            gold = jnp.where(gold_owner == owner, gold_row, -1.0).astype(jnp.int32)
            share = share_ref[0:1, pl.ds(at, rows)]
            if h == 1:
                share = jnp.where(early, share, share_ref[1:2, pl.ds(at, rows)])
            weights = share * exp_ref[s]
            grad = (weights - jnp.where(ids == gold, 1.0, 0.0)).astype(bf16)
            line = pl.ds(pl.multiple_of(place * BLOCK, BLOCK), BLOCK)
            g_ref[s, line, :] = grad
            grad_ref[line, s * rows : (s + 1) * rows] = grad
    part = jnp.dot(grad_ref[...], rows_ref[...], preferred_element_type=f32)
    type_ref[...] = (factor * part).astype(bf16)


def mention_kernel(factor_ref, place_ref, g_ref, near_ref, *refs):
    other_refs, out_refs, tile_ref = refs[:4], refs[4 : 4 + X_SIZE], refs[-1]
    step = pl.program_id(0)

    @pl.when(step == 0)
    def _():
        join_types(place_ref, near_ref, other_refs, tile_ref)

    part = lax.dot_general(
        g_ref[0], tile_ref[...], (((0,), (0,)), ((), ())), preferred_element_type=f32
    )
    part = (factor_ref[0] * part).astype(bf16)
    for s, out_ref in enumerate(out_refs):

        @pl.when(step == s)
        def _(out_ref=out_ref):
            out_ref[...] = part


def adam_rows(type_table, adam_m, adam_v, type_grad):
    moment_one = beta_one * adam_m + (1.0 - beta_one) * type_grad
    moment_two = beta_two * adam_v + (1.0 - beta_two) * type_grad * type_grad
    updated = type_table - learn_rate * (moment_one / first_fix) / (
        jnp.sqrt(moment_two / second_fix) + adam_eps
    )
    return (updated, moment_one, moment_two)


def params(mib=60):
    return pltpu.CompilerParams(vmem_limit_bytes=mib * 1024 * 1024)


def paired(array, axis, partner):
    return lax.ppermute(array, axis, [(i, partner(i)) for i in range(lax.axis_size(axis))])


def per_device(
    mentions,
    type_table,
    adam_m,
    adam_v,
    logit_scale,
    block_lists,
    list_lengths,
    gold_slot,
    gold_row,
):
    cols = lax.axis_size("gy")
    devices = Z_SIZE * X_SIZE * cols
    block_rows, width = type_table.shape
    rows = mentions.shape[0]
    sent_rows = rows + META_ROWS
    types = Z_SIZE * block_rows
    smem = pl.BlockSpec(memory_space=pltpu.SMEM)
    hbm = pl.BlockSpec(memory_space=pltpu.HBM)
    place = jnp.stack([lax.axis_index("gz"), lax.axis_index("gx")]).astype(jnp.int32)
    half = Z_SIZE // 2

    def tile(*shape):
        return pl.BlockSpec((1,) + shape, lambda j: (j, 0, 0))

    def whole(*shape):
        return pl.BlockSpec(shape, lambda j: (0,) * len(shape))

    own, copies = pl.pallas_call(
        cast_kernel,
        out_shape=[
            jax.ShapeDtypeStruct((block_rows, width), bf16),
            jax.ShapeDtypeStruct((half, block_rows, width), bf16),
        ],
        compiler_params=params(),
        name="cast",
    )(type_table)
    parities = [list(range(p, Z_SIZE, 2)) for p in range(2)]
    near = lax.all_to_all(copies, "gz", 0, 0, tiled=True, axis_index_groups=parities)
    pairings = [lambda z: z ^ 1, lambda z: ((z + 1) ^ 1) - 1 & Z_SIZE - 1]
    one, two = [paired(own, "gz", pairing) for pairing in pairings]
    _, order = other_blocks(place)
    index = lax.div(place[0], 2)
    sent = [lax.rem(2 * index - k + half, half) for k in order[2:0:-1]]
    low, high = [
        paired(lax.dynamic_index_in_dim(near, k, 0, keepdims=False), "gz", pairing)
        for k, pairing in zip(sent, pairings)
    ]
    others = (one, two, low, high)
    near_spec = whole(half, block_rows, width)
    block_spec = whole(block_rows, width)
    packed = pl.pallas_call(
        lambda *refs: pack_kernel(cols, *refs),
        in_specs=[hbm] * 5,
        out_shape=jax.ShapeDtypeStruct((sent_rows, width), bf16),
        scratch_shapes=[
            pltpu.VMEM((2, SLOTS), jnp.int32),
            pltpu.VMEM((1, 2), jnp.int32),
            pltpu.VMEM((1, rows), jnp.int32),
            pltpu.VMEM((1, rows), jnp.int32),
            pltpu.SemaphoreType.DMA((5,)),
        ],
        compiler_params=params(),
        name="pack",
    )(
        block_lists,
        list_lengths.reshape(1, 2),
        gold_slot.reshape(1, rows),
        gold_row.reshape(1, rows),
        mentions,
    )
    gathered = jnp.stack(
        [packed] + [paired(packed, "gx", lambda x, s=s: x ^ s) for s in range(1, X_SIZE)]
    )

    half_types = half * block_rows
    mid_types = 2 * block_rows
    exps_shape = jax.ShapeDtypeStruct((X_SIZE, half_types, rows), f32)

    def scratch(types):
        return [pltpu.VMEM((types, width), bf16), pltpu.VMEM((types, rows), f32)]

    near_exps, mid_exps, near_stats = pl.pallas_call(
        near_kernel,
        grid=(X_SIZE,),
        in_specs=[smem, smem, tile(sent_rows, width), near_spec] + [block_spec] * 2,
        out_specs=[tile(half_types, rows), tile(mid_types, rows), tile(STAT_ROWS, rows)],
        out_shape=[
            exps_shape,
            jax.ShapeDtypeStruct((X_SIZE, mid_types, rows), f32),
            jax.ShapeDtypeStruct((X_SIZE, STAT_ROWS, rows), f32),
        ],
        scratch_shapes=scratch(half_types + mid_types),
        compiler_params=params(16),
        name="near_scores",
    )(logit_scale, place, gathered, near, one, two)
    far_exps, stats = pl.pallas_call(
        far_kernel,
        grid=(X_SIZE,),
        in_specs=[smem, smem, tile(sent_rows, width)]
        + [block_spec] * 2
        + [tile(mid_types, rows), tile(STAT_ROWS, rows)],
        out_specs=[tile(half_types, rows), whole(X_SIZE, STAT_ROWS, X_SIZE * rows)],
        out_shape=[exps_shape, jax.ShapeDtypeStruct((X_SIZE, STAT_ROWS, X_SIZE * rows), f32)],
        scratch_shapes=scratch(mid_types),
        compiler_params=params(16),
        name="far_scores",
    )(logit_scale, place, gathered, low, high, mid_exps, near_stats)
    stats = lax.all_to_all(stats, "gx", 0, 0, tiled=True)
    chunk = 2 * block_rows
    chunk_spec = pl.BlockSpec((X_SIZE, chunk, rows), lambda i: (0, i, 0))
    grads, type_part, scale_parts = pl.pallas_call(
        grads_kernel,
        grid=(types // chunk,),
        in_specs=[
            smem,
            smem,
            pl.BlockSpec((X_SIZE, block_rows, rows), lambda i: (0, i, 0)),
            pl.BlockSpec((X_SIZE, block_rows, rows), lambda i: (0, i, 0)),
            whole(X_SIZE, STAT_ROWS, X_SIZE * rows),
            whole(X_SIZE, sent_rows, width),
        ],
        out_specs=[chunk_spec, pl.BlockSpec((chunk, width), lambda i: (i, 0)), whole(Z_SIZE * cols, 1, 128)],
        out_shape=[
            jax.ShapeDtypeStruct((X_SIZE, types, rows), bf16),
            jax.ShapeDtypeStruct((types, width), bf16),
            jax.ShapeDtypeStruct((Z_SIZE * cols, 1, 128), f32),
        ],
        scratch_shapes=[
            pltpu.VMEM((2, X_SIZE * rows), f32),
            pltpu.VMEM((X_SIZE * rows, width), bf16),
            pltpu.VMEM((chunk, X_SIZE * rows), bf16),
        ],
        compiler_params=params(16),
        name="grads",
    )(logit_scale, place, near_exps, far_exps, stats, gathered)
    type_grad = lax.psum_scatter(type_part, "gz", scatter_dimension=0, tiled=True)
    parts = pl.pallas_call(
        mention_kernel,
        grid=(X_SIZE,),
        in_specs=[smem, smem, tile(types, rows), near_spec] + [block_spec] * 4,
        out_specs=[whole(rows, width)] * X_SIZE,
        out_shape=[jax.ShapeDtypeStruct((rows, width), bf16)] * X_SIZE,
        scratch_shapes=[pltpu.VMEM((types, width), bf16)],
        compiler_params=params(16),
        name="mention_part",
    )(logit_scale, place, grads, near, *others)
    mention_grad = parts[0].astype(f32)
    for s in range(1, X_SIZE):
        mention_grad = mention_grad + paired(
            parts[s], "gx", lambda x, s=s: x ^ s
        ).astype(f32)
    mention_grad = mention_grad.astype(bf16)
    scale_parts = lax.all_to_all(scale_parts, ("gz", "gy"), 0, 0, tiled=True)
    scale_grad = (jnp.sum(scale_parts[:, 0, 0]) / (rows * devices)).reshape(1)
    new_table, new_first, new_second = adam_rows(
        type_table, adam_m, adam_v, type_grad.astype(f32)
    )
    return (new_table, new_first, new_second, mention_grad, scale_grad)


def solution(mesh):
    gx, gy = mesh.devices.shape
    split = Mesh(mesh.devices.reshape(gx // X_SIZE, X_SIZE, gy), ("gz", "gx", "gy"))
    axes = ("gz", "gx", "gy")
    rows = P(axes, None)
    return jax.shard_map(
        per_device,
        mesh=split,
        in_specs=(rows, rows, rows, rows, P(), rows, P(axes), P(axes), P(axes)),
        out_specs=(rows, rows, rows, rows, P()),
        check_vma=False,
    )
```

```python
import jax
import jax.numpy as jnp
from jax import lax
from jax.experimental import pallas as pl
from jax.experimental.pallas import tpu as pltpu
from jax.sharding import Mesh, PartitionSpec as P

beta_one = 0.9
beta_two = 0.999
learn_rate = 0.02
adam_eps = 1e-08
first_fix = 0.9999734386011124
second_fix = 0.09520785288629038

X_SIZE = 4
Z_SIZE = 8
BLOCK = 128
LOW = -1e30
META_ROWS = 32
SLOTS = 16
STAT_ROWS = 8
SCALE_LANES = 768
f32 = jnp.float32
bf16 = jnp.bfloat16


def cast_kernel(t_ref, out_ref):
    block = t_ref[...].astype(bf16)
    for k in range(out_ref.shape[0]):
        out_ref[k] = block


def pack_kernel(
    cols, list_hbm, len_hbm, slot_hbm, row_hbm, m_hbm, out_ref, list_ref, len_ref, slot_ref, row_ref, sems
):
    rows, width = m_hbm.shape
    pairs = [(list_hbm, list_ref), (len_hbm, len_ref), (slot_hbm, slot_ref), (row_hbm, row_ref)]
    pairs.append((m_hbm, out_ref.at[pl.ds(0, rows), :]))
    copies = [pltpu.make_async_copy(src, dst, sems.at[i]) for i, (src, dst) in enumerate(pairs)]
    for copy in copies:
        copy.start()
    for copy in copies[:4]:
        copy.wait()
    owners = lax.div(list_ref[...], cols).astype(f32)
    lens = len_ref[...]
    first = lax.broadcasted_iota(jnp.int32, (1, rows), 1) < BLOCK
    length = jnp.where(first, lens[:, 0:1], lens[:, 1:2])
    slot = slot_ref[...]
    gold = jnp.zeros((1, rows), f32)
    lines = []
    for k in range(SLOTS):
        owner = jnp.where(first, owners[0:1, k : k + 1], owners[1:2, k : k + 1])
        gold = gold + jnp.where(slot == k, owner, 0.0)
        lines.append(jnp.where(length > k, owner, -1.0))
    lines += [gold, row_ref[...].astype(f32)]
    lines.append(jnp.zeros((META_ROWS - len(lines), rows), f32))
    out_ref[rows : rows + META_ROWS, :] = jnp.zeros((META_ROWS, width), bf16)
    out_ref[rows : rows + META_ROWS, 0:rows] = jnp.concatenate(lines, axis=0).astype(bf16)
    copies[4].wait()


def owner_at(place_ref, line):
    return (line * X_SIZE + place_ref[1]).astype(f32)


def tile_from(place_ref, step):
    return jnp.bitwise_xor(place_ref[1], step)


def join_types(place_ref, near_ref, low_ref, high_ref, tile_ref):
    parity = lax.rem(place_ref[0], 2)
    half = Z_SIZE // 4
    for k in range(Z_SIZE // 2):
        other = low_ref[k] if k < half else high_ref[k - half]
        tile_ref[pl.ds(pl.multiple_of((2 * k + parity) * BLOCK, BLOCK), BLOCK), :] = near_ref[k]
        tile_ref[pl.ds(pl.multiple_of((2 * k + 1 - parity) * BLOCK, BLOCK), BLOCK), :] = other


def score_half(factor, place_ref, shift, m_ref, tile_ref, raw_ref, exp_ref):
    rows = m_ref.shape[1] - META_ROWS
    raw_ref[...] = lax.dot_general(
        tile_ref[...], m_ref[0, 0:rows, :], (((1,), (1,)), ((), ())), preferred_element_type=f32
    )
    meta = m_ref[0, rows : rows + META_ROWS, 0:rows].astype(f32)
    owners = meta[0:SLOTS, :]
    gold_owner = meta[SLOTS : SLOTS + 1, :]
    gold_row = meta[SLOTS + 1 : SLOTS + 2, :].astype(jnp.int32)
    ids = lax.broadcasted_iota(jnp.int32, (BLOCK, rows), 0)
    top = jnp.full((1, rows), LOW, f32)
    gold_raw = jnp.zeros((1, rows), f32)
    lives = []
    for k in range(Z_SIZE // 2):
        owner = owner_at(place_ref, 2 * k + shift)
        lives.append(jnp.max(jnp.where(owners == owner, 1.0, 0.0), axis=0, keepdims=True) > 0.0)
        raw = raw_ref[k * BLOCK : (k + 1) * BLOCK, :]
        top = jnp.maximum(top, jnp.where(lives[k], jnp.max(raw, axis=0, keepdims=True), LOW))
        gold = jnp.where(gold_owner == owner, gold_row, -1)
        gold_raw = gold_raw + jnp.sum(jnp.where(ids == gold, raw, 0.0), axis=0, keepdims=True)
    total = jnp.zeros((1, rows), f32)
    mass = jnp.zeros((1, rows), f32)
    for k in range(Z_SIZE // 2):
        below = jnp.where(lives[k], top, -LOW)
        gap = raw_ref[k * BLOCK : (k + 1) * BLOCK, :] - below
        weights = jnp.exp(factor * gap)
        exp_ref[0, k * BLOCK : (k + 1) * BLOCK, :] = weights
        total = total + jnp.sum(weights, axis=0, keepdims=True)
        mass = mass + jnp.sum(weights * gap, axis=0, keepdims=True)
    return top, total, mass, gold_raw


def near_kernel(factor_ref, place_ref, m_ref, near_ref, exp_ref, stat_ref, tile_ref, raw_ref):
    step = pl.program_id(0)

    @pl.when(step == 0)
    def _():
        for k in range(near_ref.shape[0]):
            tile_ref[k * BLOCK : (k + 1) * BLOCK, :] = near_ref[k]

    shift = lax.rem(place_ref[0], 2)
    stats = score_half(factor_ref[0], place_ref, shift, m_ref, tile_ref, raw_ref, exp_ref)
    rows = stats[0].shape[1]
    rest = jnp.zeros((STAT_ROWS - len(stats), rows), f32)
    stat_ref[0] = jnp.concatenate(list(stats) + [rest], axis=0)


def far_kernel(
    factor_ref, place_ref, m_ref, low_ref, high_ref, part_ref, exp_ref, stat_ref, tile_ref, raw_ref
):
    step = pl.program_id(0)

    @pl.when(step == 0)
    def _():
        half = low_ref.shape[0]
        for k in range(2 * half):
            other = low_ref[k] if k < half else high_ref[k - half]
            tile_ref[k * BLOCK : (k + 1) * BLOCK, :] = other

    shift = 1 - lax.rem(place_ref[0], 2)
    top, total, mass, gold_raw = score_half(
        factor_ref[0], place_ref, shift, m_ref, tile_ref, raw_ref, exp_ref
    )
    rows = top.shape[1]
    near = part_ref[0]
    lines = [near[0:3, :], top, total, mass, gold_raw + near[3:4, :]]
    lines.append(jnp.zeros((STAT_ROWS - 7, rows), f32))
    stat = jnp.concatenate(lines, axis=0)
    at = pl.multiple_of(tile_from(place_ref, step) * rows, BLOCK)
    for d in range(stat_ref.shape[0]):
        stat_ref[d, :, pl.ds(at, rows)] = stat


def merge_stats(factor, place_ref, stat_ref, share_ref, scale_ref):
    tops, sums, masses = [
        jnp.concatenate([stat_ref[:, r, :], stat_ref[:, r + 3, :]], axis=0) for r in range(3)
    ]
    top = jnp.max(tops, axis=0, keepdims=True)
    shares = jnp.exp(factor * (tops - top))
    total = jnp.sum(sums * shares, axis=0, keepdims=True)
    masses = masses + sums * tops
    mass = jnp.sum(jnp.where(sums > 0.0, masses * shares, 0.0), axis=0, keepdims=True)
    scale = mass / total - jnp.sum(stat_ref[:, 6, :], axis=0, keepdims=True)
    scale = jnp.sum(scale, axis=1, keepdims=True)
    scale_ref[...] = jnp.broadcast_to(scale[None], scale_ref.shape)
    ids = lax.broadcasted_iota(jnp.int32, tops.shape, 0)
    for h in range(2):
        mine = ids == place_ref[1] + h * X_SIZE
        own = jnp.max(jnp.where(mine, tops, LOW), axis=0, keepdims=True)
        share_ref[h : h + 1, :] = jnp.exp(factor * (own - top) - jnp.log(total))


def grads_kernel(
    factor_ref, place_ref, near_ref, far_ref, stat_ref, m_ref, g_ref, type_ref, scale_ref, share_ref, rows_ref, grad_ref
):
    step = pl.program_id(0)
    factor = factor_ref[0]
    rows = m_ref.shape[1] - META_ROWS

    @pl.when(step == 0)
    def _():
        merge_stats(factor, place_ref, stat_ref, share_ref, scale_ref)
        for s in range(X_SIZE):
            rows_ref[s * rows : (s + 1) * rows, :] = m_ref[s, 0:rows, :]

    ids = lax.broadcasted_iota(jnp.int32, (BLOCK, rows), 0)
    parity = lax.rem(place_ref[0], 2)
    for s in range(X_SIZE):
        at = pl.multiple_of(tile_from(place_ref, s) * rows, BLOCK)
        meta = m_ref[s, rows + SLOTS : rows + META_ROWS, 0:rows].astype(f32)
        gold_owner = meta[0:1, :]
        gold_row = meta[1:2, :]
        for h, exp_ref in enumerate((near_ref, far_ref)):
            place = parity if h == 0 else 1 - parity
            owner = owner_at(place_ref, 2 * step + place)
            gold = jnp.where(gold_owner == owner, gold_row, -1.0).astype(jnp.int32)
            weights = share_ref[h : h + 1, pl.ds(at, rows)] * exp_ref[s]
            grad = (weights - jnp.where(ids == gold, 1.0, 0.0)).astype(bf16)
            line = pl.ds(pl.multiple_of(place * BLOCK, BLOCK), BLOCK)
            g_ref[s, line, :] = grad
            grad_ref[line, s * rows : (s + 1) * rows] = grad
    part = jnp.dot(grad_ref[...], rows_ref[...], preferred_element_type=f32)
    type_ref[...] = (factor * part).astype(bf16)


def mention_kernel(factor_ref, place_ref, g_ref, near_ref, low_ref, high_ref, *refs):
    out_refs, tile_ref = refs[:X_SIZE], refs[-1]
    step = pl.program_id(0)

    @pl.when(step == 0)
    def _():
        join_types(place_ref, near_ref, low_ref, high_ref, tile_ref)

    part = lax.dot_general(
        g_ref[0], tile_ref[...], (((0,), (0,)), ((), ())), preferred_element_type=f32
    )
    part = (factor_ref[0] * part).astype(bf16)
    for s, out_ref in enumerate(out_refs):

        @pl.when(step == s)
        def _(out_ref=out_ref):
            out_ref[...] = part


def adam_rows(type_table, adam_m, adam_v, type_grad):
    moment_one = beta_one * adam_m + (1.0 - beta_one) * type_grad
    moment_two = beta_two * adam_v + (1.0 - beta_two) * type_grad * type_grad
    updated = type_table - learn_rate * (moment_one / first_fix) / (
        jnp.sqrt(moment_two / second_fix) + adam_eps
    )
    return (updated, moment_one, moment_two)


def params(mib=60):
    return pltpu.CompilerParams(vmem_limit_bytes=mib * 1024 * 1024)


def paired(array, axis, partner):
    return lax.ppermute(array, axis, [(i, partner(i)) for i in range(lax.axis_size(axis))])


def per_device(
    mentions,
    type_table,
    adam_m,
    adam_v,
    logit_scale,
    block_lists,
    list_lengths,
    gold_slot,
    gold_row,
):
    cols = lax.axis_size("gy")
    devices = Z_SIZE * X_SIZE * cols
    block_rows, width = type_table.shape
    rows = mentions.shape[0]
    sent_rows = rows + META_ROWS
    types = Z_SIZE * block_rows
    smem = pl.BlockSpec(memory_space=pltpu.SMEM)
    hbm = pl.BlockSpec(memory_space=pltpu.HBM)
    place = jnp.stack([lax.axis_index("gz"), lax.axis_index("gx")]).astype(jnp.int32)
    half = Z_SIZE // 2

    def tile(*shape):
        return pl.BlockSpec((1,) + shape, lambda j: (j, 0, 0))

    def whole(*shape):
        return pl.BlockSpec(shape, lambda j: (0,) * len(shape))

    copies = pl.pallas_call(
        cast_kernel,
        out_shape=jax.ShapeDtypeStruct((half, block_rows, width), bf16),
        compiler_params=params(),
        name="cast",
    )(type_table)
    parities = [list(range(p, Z_SIZE, 2)) for p in range(2)]
    near = lax.all_to_all(copies, "gz", 0, 0, tiled=True, axis_index_groups=parities)
    low = paired(near[: half // 2], "gz", lambda z: z ^ 1)
    high = paired(near[half // 2 :], "gz", lambda z: ((z + 1) ^ 1) - 1 & Z_SIZE - 1)
    table = (near, low, high)
    table_specs = [whole(t.shape[0], block_rows, width) for t in table]
    packed = pl.pallas_call(
        lambda *refs: pack_kernel(cols, *refs),
        in_specs=[hbm] * 5,
        out_shape=jax.ShapeDtypeStruct((sent_rows, width), bf16),
        scratch_shapes=[
            pltpu.VMEM((2, SLOTS), jnp.int32),
            pltpu.VMEM((1, 2), jnp.int32),
            pltpu.VMEM((1, rows), jnp.int32),
            pltpu.VMEM((1, rows), jnp.int32),
            pltpu.SemaphoreType.DMA((5,)),
        ],
        compiler_params=params(),
        name="pack",
    )(
        block_lists,
        list_lengths.reshape(1, 2),
        gold_slot.reshape(1, rows),
        gold_row.reshape(1, rows),
        mentions,
    )
    gathered = jnp.stack(
        [packed] + [paired(packed, "gx", lambda x, s=s: x ^ s) for s in range(1, X_SIZE)]
    )

    half_types = half * block_rows
    scratch = [pltpu.VMEM((half_types, width), bf16), pltpu.VMEM((half_types, rows), f32)]
    exps_shape = jax.ShapeDtypeStruct((X_SIZE, half_types, rows), f32)
    near_exps, near_stats = pl.pallas_call(
        near_kernel,
        grid=(X_SIZE,),
        in_specs=[smem, smem, tile(sent_rows, width)] + table_specs[:1],
        out_specs=[tile(half_types, rows), tile(STAT_ROWS, rows)],
        out_shape=[exps_shape, jax.ShapeDtypeStruct((X_SIZE, STAT_ROWS, rows), f32)],
        scratch_shapes=scratch,
        compiler_params=params(16),
        name="near_scores",
    )(logit_scale, place, gathered, near)
    far_exps, stats = pl.pallas_call(
        far_kernel,
        grid=(X_SIZE,),
        in_specs=[smem, smem, tile(sent_rows, width)] + table_specs[1:] + [tile(STAT_ROWS, rows)],
        out_specs=[tile(half_types, rows), whole(X_SIZE, STAT_ROWS, X_SIZE * rows)],
        out_shape=[exps_shape, jax.ShapeDtypeStruct((X_SIZE, STAT_ROWS, X_SIZE * rows), f32)],
        scratch_shapes=scratch,
        compiler_params=params(16),
        name="far_scores",
    )(logit_scale, place, gathered, low, high, near_stats)
    stats = lax.all_to_all(stats, "gx", 0, 0, tiled=True)
    chunk = 2 * block_rows
    scale_shape = (Z_SIZE * cols, 1, SCALE_LANES)
    chunk_spec = pl.BlockSpec((X_SIZE, chunk, rows), lambda i: (0, i, 0))
    grads, type_part, scale_parts = pl.pallas_call(
        grads_kernel,
        grid=(types // chunk,),
        in_specs=[
            smem,
            smem,
            pl.BlockSpec((X_SIZE, block_rows, rows), lambda i: (0, i, 0)),
            pl.BlockSpec((X_SIZE, block_rows, rows), lambda i: (0, i, 0)),
            whole(X_SIZE, STAT_ROWS, X_SIZE * rows),
            whole(X_SIZE, sent_rows, width),
        ],
        out_specs=[chunk_spec, pl.BlockSpec((chunk, width), lambda i: (i, 0)), whole(*scale_shape)],
        out_shape=[
            jax.ShapeDtypeStruct((X_SIZE, types, rows), bf16),
            jax.ShapeDtypeStruct((types, width), bf16),
            jax.ShapeDtypeStruct(scale_shape, f32),
        ],
        scratch_shapes=[
            pltpu.VMEM((2, X_SIZE * rows), f32),
            pltpu.VMEM((X_SIZE * rows, width), bf16),
            pltpu.VMEM((chunk, X_SIZE * rows), bf16),
        ],
        compiler_params=params(16),
        name="grads",
    )(logit_scale, place, near_exps, far_exps, stats, gathered)
    type_grad = lax.psum_scatter(type_part, "gz", scatter_dimension=0, tiled=True)
    parts = pl.pallas_call(
        mention_kernel,
        grid=(X_SIZE,),
        in_specs=[smem, smem, tile(types, rows)] + table_specs,
        out_specs=[whole(rows, width)] * X_SIZE,
        out_shape=[jax.ShapeDtypeStruct((rows, width), bf16)] * X_SIZE,
        scratch_shapes=[pltpu.VMEM((types, width), bf16)],
        compiler_params=params(16),
        name="mention_part",
    )(logit_scale, place, grads, *table)
    mention_grad = parts[0].astype(f32)
    for s in range(1, X_SIZE):
        mention_grad = mention_grad + paired(
            parts[s], "gx", lambda x, s=s: x ^ s
        ).astype(f32)
    mention_grad = mention_grad.astype(bf16)
    scale_parts = lax.all_to_all(scale_parts, ("gz", "gy"), 0, 0, tiled=True)
    scale_grad = (jnp.sum(scale_parts[:, 0, 0]) / (rows * devices)).reshape(1)
    new_table, new_first, new_second = adam_rows(
        type_table, adam_m, adam_v, type_grad.astype(f32)
    )
    return (new_table, new_first, new_second, mention_grad, scale_grad)


def solution(mesh):
    gx, gy = mesh.devices.shape
    split = Mesh(mesh.devices.reshape(gx // X_SIZE, X_SIZE, gy), ("gz", "gx", "gy"))
    axes = ("gz", "gx", "gy")
    rows = P(axes, None)
    return jax.shard_map(
        per_device,
        mesh=split,
        in_specs=(rows, rows, rows, rows, P(), rows, P(axes), P(axes), P(axes)),
        out_specs=(rows, rows, rows, rows, P()),
        check_vma=False,
    )
```

```python
import jax
import jax.numpy as jnp
from jax import lax
from jax.experimental import pallas as pl
from jax.experimental.pallas import tpu as pltpu
from jax.sharding import Mesh, PartitionSpec as P

beta_one = 0.9
beta_two = 0.999
learn_rate = 0.02
adam_eps = 1e-08
first_fix = 0.9999734386011124
second_fix = 0.09520785288629038

X_SIZE = 4
Z_SIZE = 8
BLOCK = 128
LOW = -1e30
META_ROWS = 32
SLOTS = 16
STAT_ROWS = 8
f32 = jnp.float32
bf16 = jnp.bfloat16


def cast_kernel(t_ref, out_ref):
    block = t_ref[...].astype(bf16)
    for k in range(out_ref.shape[0]):
        out_ref[k] = block


def pack_kernel(
    cols, list_hbm, len_hbm, slot_hbm, row_hbm, m_hbm, out_ref, list_ref, len_ref, slot_ref, row_ref, sems
):
    rows, width = m_hbm.shape
    pairs = [(list_hbm, list_ref), (len_hbm, len_ref), (slot_hbm, slot_ref), (row_hbm, row_ref)]
    pairs.append((m_hbm, out_ref.at[pl.ds(0, rows), :]))
    copies = [pltpu.make_async_copy(src, dst, sems.at[i]) for i, (src, dst) in enumerate(pairs)]
    for copy in copies:
        copy.start()
    for copy in copies[:4]:
        copy.wait()
    owners = lax.div(list_ref[...], cols).astype(f32)
    lens = len_ref[...]
    first = lax.broadcasted_iota(jnp.int32, (1, rows), 1) < BLOCK
    length = jnp.where(first, lens[:, 0:1], lens[:, 1:2])
    slot = slot_ref[...]
    gold = jnp.zeros((1, rows), f32)
    lines = []
    for k in range(SLOTS):
        owner = jnp.where(first, owners[0:1, k : k + 1], owners[1:2, k : k + 1])
        gold = gold + jnp.where(slot == k, owner, 0.0)
        lines.append(jnp.where(length > k, owner, -1.0))
    lines += [gold, row_ref[...].astype(f32)]
    lines.append(jnp.zeros((META_ROWS - len(lines), rows), f32))
    out_ref[rows : rows + META_ROWS, :] = jnp.zeros((META_ROWS, width), bf16)
    out_ref[rows : rows + META_ROWS, 0:rows] = jnp.concatenate(lines, axis=0).astype(bf16)
    copies[4].wait()


def owner_at(place_ref, line):
    return (line * X_SIZE + place_ref[1]).astype(f32)


def tile_from(place_ref, step):
    return jnp.bitwise_xor(place_ref[1], step)


def join_types(place_ref, near_ref, low_ref, high_ref, tile_ref):
    parity = lax.rem(place_ref[0], 2)
    half = Z_SIZE // 4
    for k in range(Z_SIZE // 2):
        other = low_ref[k] if k < half else high_ref[k - half]
        tile_ref[pl.ds(pl.multiple_of((2 * k + parity) * BLOCK, BLOCK), BLOCK), :] = near_ref[k]
        tile_ref[pl.ds(pl.multiple_of((2 * k + 1 - parity) * BLOCK, BLOCK), BLOCK), :] = other


def score_half(factor, place_ref, shift, m_ref, tile_ref, raw_ref, exp_ref):
    rows = m_ref.shape[1] - META_ROWS
    raw_ref[...] = lax.dot_general(
        tile_ref[...], m_ref[0, 0:rows, :], (((1,), (1,)), ((), ())), preferred_element_type=f32
    )
    meta = m_ref[0, rows : rows + META_ROWS, 0:rows].astype(f32)
    owners = meta[0:SLOTS, :]
    gold_owner = meta[SLOTS : SLOTS + 1, :]
    gold_row = meta[SLOTS + 1 : SLOTS + 2, :].astype(jnp.int32)
    ids = lax.broadcasted_iota(jnp.int32, (BLOCK, rows), 0)
    top = jnp.full((1, rows), LOW, f32)
    gold_raw = jnp.zeros((1, rows), f32)
    lives = []
    for k in range(Z_SIZE // 2):
        owner = owner_at(place_ref, 2 * k + shift)
        lives.append(jnp.max(jnp.where(owners == owner, 1.0, 0.0), axis=0, keepdims=True) > 0.0)
        raw = raw_ref[k * BLOCK : (k + 1) * BLOCK, :]
        top = jnp.maximum(top, jnp.where(lives[k], jnp.max(raw, axis=0, keepdims=True), LOW))
        gold = jnp.where(gold_owner == owner, gold_row, -1)
        gold_raw = gold_raw + jnp.sum(jnp.where(ids == gold, raw, 0.0), axis=0, keepdims=True)
    total = jnp.zeros((1, rows), f32)
    mass = jnp.zeros((1, rows), f32)
    for k in range(Z_SIZE // 2):
        below = jnp.where(lives[k], top, -LOW)
        gap = raw_ref[k * BLOCK : (k + 1) * BLOCK, :] - below
        weights = jnp.exp(factor * gap)
        exp_ref[0, k * BLOCK : (k + 1) * BLOCK, :] = weights
        total = total + jnp.sum(weights, axis=0, keepdims=True)
        mass = mass + jnp.sum(weights * gap, axis=0, keepdims=True)
    return top, total, mass, gold_raw


def near_kernel(factor_ref, place_ref, m_ref, near_ref, exp_ref, stat_ref, tile_ref, raw_ref):
    step = pl.program_id(0)

    @pl.when(step == 0)
    def _():
        for k in range(near_ref.shape[0]):
            tile_ref[k * BLOCK : (k + 1) * BLOCK, :] = near_ref[k]

    shift = lax.rem(place_ref[0], 2)
    stats = score_half(factor_ref[0], place_ref, shift, m_ref, tile_ref, raw_ref, exp_ref)
    rows = stats[0].shape[1]
    rest = jnp.zeros((STAT_ROWS - len(stats), rows), f32)
    stat_ref[0] = jnp.concatenate(list(stats) + [rest], axis=0)


def far_kernel(
    factor_ref, place_ref, m_ref, low_ref, high_ref, part_ref, exp_ref, stat_ref, tile_ref, raw_ref
):
    step = pl.program_id(0)

    @pl.when(step == 0)
    def _():
        half = low_ref.shape[0]
        for k in range(2 * half):
            other = low_ref[k] if k < half else high_ref[k - half]
            tile_ref[k * BLOCK : (k + 1) * BLOCK, :] = other

    shift = 1 - lax.rem(place_ref[0], 2)
    top, total, mass, gold_raw = score_half(
        factor_ref[0], place_ref, shift, m_ref, tile_ref, raw_ref, exp_ref
    )
    rows = top.shape[1]
    near = part_ref[0]
    lines = [near[0:3, :], top, total, mass, gold_raw + near[3:4, :]]
    lines.append(jnp.zeros((STAT_ROWS - 7, rows), f32))
    stat = jnp.concatenate(lines, axis=0)
    at = pl.multiple_of(tile_from(place_ref, step) * rows, BLOCK)
    for d in range(stat_ref.shape[0]):
        stat_ref[d, :, pl.ds(at, rows)] = stat


def merge_stats(factor, place_ref, stat_ref, share_ref, scale_ref):
    tops, sums, masses = [
        jnp.concatenate([stat_ref[:, r, :], stat_ref[:, r + 3, :]], axis=0) for r in range(3)
    ]
    top = jnp.max(tops, axis=0, keepdims=True)
    shares = jnp.exp(factor * (tops - top))
    total = jnp.sum(sums * shares, axis=0, keepdims=True)
    masses = masses + sums * tops
    mass = jnp.sum(jnp.where(sums > 0.0, masses * shares, 0.0), axis=0, keepdims=True)
    scale = mass / total - jnp.sum(stat_ref[:, 6, :], axis=0, keepdims=True)
    scale_ref[...] = jnp.broadcast_to(jnp.sum(scale, axis=1, keepdims=True), scale_ref.shape)
    ids = lax.broadcasted_iota(jnp.int32, tops.shape, 0)
    for h in range(2):
        mine = ids == place_ref[1] + h * X_SIZE
        own = jnp.max(jnp.where(mine, tops, LOW), axis=0, keepdims=True)
        share_ref[h : h + 1, :] = jnp.exp(factor * (own - top) - jnp.log(total))


def grads_kernel(
    factor_ref, place_ref, near_ref, far_ref, stat_ref, m_ref, g_ref, type_ref, scale_ref, share_ref, rows_ref, grad_ref
):
    step = pl.program_id(0)
    factor = factor_ref[0]
    rows = m_ref.shape[1] - META_ROWS

    @pl.when(step == 0)
    def _():
        merge_stats(factor, place_ref, stat_ref, share_ref, scale_ref)
        for s in range(X_SIZE):
            rows_ref[s * rows : (s + 1) * rows, :] = m_ref[s, 0:rows, :]

    ids = lax.broadcasted_iota(jnp.int32, (BLOCK, rows), 0)
    parity = lax.rem(place_ref[0], 2)
    for s in range(X_SIZE):
        at = pl.multiple_of(tile_from(place_ref, s) * rows, BLOCK)
        meta = m_ref[s, rows + SLOTS : rows + META_ROWS, 0:rows].astype(f32)
        gold_owner = meta[0:1, :]
        gold_row = meta[1:2, :]
        for h, exp_ref in enumerate((near_ref, far_ref)):
            place = parity if h == 0 else 1 - parity
            owner = owner_at(place_ref, 2 * step + place)
            gold = jnp.where(gold_owner == owner, gold_row, -1.0).astype(jnp.int32)
            weights = share_ref[h : h + 1, pl.ds(at, rows)] * exp_ref[s]
            grad = (weights - jnp.where(ids == gold, 1.0, 0.0)).astype(bf16)
            line = pl.ds(pl.multiple_of(place * BLOCK, BLOCK), BLOCK)
            g_ref[s, line, :] = grad
            grad_ref[line, s * rows : (s + 1) * rows] = grad
    part = jnp.dot(grad_ref[...], rows_ref[...], preferred_element_type=f32)
    type_ref[...] = (factor * part).astype(bf16)


def mention_kernel(factor_ref, place_ref, g_ref, near_ref, low_ref, high_ref, *refs):
    out_refs, tile_ref = refs[:X_SIZE], refs[-1]
    step = pl.program_id(0)

    @pl.when(step == 0)
    def _():
        join_types(place_ref, near_ref, low_ref, high_ref, tile_ref)

    part = lax.dot_general(
        g_ref[0], tile_ref[...], (((0,), (0,)), ((), ())), preferred_element_type=f32
    )
    part = (factor_ref[0] * part).astype(bf16)
    for s, out_ref in enumerate(out_refs):

        @pl.when(step == s)
        def _(out_ref=out_ref):
            out_ref[...] = part


def adam_rows(type_table, adam_m, adam_v, type_grad):
    moment_one = beta_one * adam_m + (1.0 - beta_one) * type_grad
    moment_two = beta_two * adam_v + (1.0 - beta_two) * type_grad * type_grad
    updated = type_table - learn_rate * (moment_one / first_fix) / (
        jnp.sqrt(moment_two / second_fix) + adam_eps
    )
    return (updated, moment_one, moment_two)


def params(mib=60):
    return pltpu.CompilerParams(vmem_limit_bytes=mib * 1024 * 1024)


def paired(array, axis, partner):
    return lax.ppermute(array, axis, [(i, partner(i)) for i in range(lax.axis_size(axis))])


def per_device(
    mentions,
    type_table,
    adam_m,
    adam_v,
    logit_scale,
    block_lists,
    list_lengths,
    gold_slot,
    gold_row,
):
    cols = lax.axis_size("gy")
    devices = Z_SIZE * X_SIZE * cols
    block_rows, width = type_table.shape
    rows = mentions.shape[0]
    sent_rows = rows + META_ROWS
    types = Z_SIZE * block_rows
    smem = pl.BlockSpec(memory_space=pltpu.SMEM)
    hbm = pl.BlockSpec(memory_space=pltpu.HBM)
    place = jnp.stack([lax.axis_index("gz"), lax.axis_index("gx")]).astype(jnp.int32)
    half = Z_SIZE // 2

    def tile(*shape):
        return pl.BlockSpec((1,) + shape, lambda j: (j, 0, 0))

    def whole(*shape):
        return pl.BlockSpec(shape, lambda j: (0,) * len(shape))

    copies = pl.pallas_call(
        cast_kernel,
        out_shape=jax.ShapeDtypeStruct((half, block_rows, width), bf16),
        compiler_params=params(),
        name="cast",
    )(type_table)
    parities = [list(range(p, Z_SIZE, 2)) for p in range(2)]
    near = lax.all_to_all(copies, "gz", 0, 0, tiled=True, axis_index_groups=parities)
    low = paired(near[: half // 2], "gz", lambda z: z ^ 1)
    high = paired(near[half // 2 :], "gz", lambda z: ((z + 1) ^ 1) - 1 & Z_SIZE - 1)
    table = (near, low, high)
    table_specs = [whole(t.shape[0], block_rows, width) for t in table]
    packed = pl.pallas_call(
        lambda *refs: pack_kernel(cols, *refs),
        in_specs=[hbm] * 5,
        out_shape=jax.ShapeDtypeStruct((sent_rows, width), bf16),
        scratch_shapes=[
            pltpu.VMEM((2, SLOTS), jnp.int32),
            pltpu.VMEM((1, 2), jnp.int32),
            pltpu.VMEM((1, rows), jnp.int32),
            pltpu.VMEM((1, rows), jnp.int32),
            pltpu.SemaphoreType.DMA((5,)),
        ],
        compiler_params=params(),
        name="pack",
    )(
        block_lists,
        list_lengths.reshape(1, 2),
        gold_slot.reshape(1, rows),
        gold_row.reshape(1, rows),
        mentions,
    )
    gathered = jnp.stack(
        [packed] + [paired(packed, "gx", lambda x, s=s: x ^ s) for s in range(1, X_SIZE)]
    )

    half_types = half * block_rows
    scratch = [pltpu.VMEM((half_types, width), bf16), pltpu.VMEM((half_types, rows), f32)]
    exps_shape = jax.ShapeDtypeStruct((X_SIZE, half_types, rows), f32)
    near_exps, near_stats = pl.pallas_call(
        near_kernel,
        grid=(X_SIZE,),
        in_specs=[smem, smem, tile(sent_rows, width)] + table_specs[:1],
        out_specs=[tile(half_types, rows), tile(STAT_ROWS, rows)],
        out_shape=[exps_shape, jax.ShapeDtypeStruct((X_SIZE, STAT_ROWS, rows), f32)],
        scratch_shapes=scratch,
        compiler_params=params(16),
        name="near_scores",
    )(logit_scale, place, gathered, near)
    far_exps, stats = pl.pallas_call(
        far_kernel,
        grid=(X_SIZE,),
        in_specs=[smem, smem, tile(sent_rows, width)] + table_specs[1:] + [tile(STAT_ROWS, rows)],
        out_specs=[tile(half_types, rows), whole(X_SIZE, STAT_ROWS, X_SIZE * rows)],
        out_shape=[exps_shape, jax.ShapeDtypeStruct((X_SIZE, STAT_ROWS, X_SIZE * rows), f32)],
        scratch_shapes=scratch,
        compiler_params=params(16),
        name="far_scores",
    )(logit_scale, place, gathered, low, high, near_stats)
    stats = lax.all_to_all(stats, "gx", 0, 0, tiled=True)
    chunk = 2 * block_rows
    chunk_spec = pl.BlockSpec((X_SIZE, chunk, rows), lambda i: (0, i, 0))
    grads, type_part, scale_part = pl.pallas_call(
        grads_kernel,
        grid=(types // chunk,),
        in_specs=[
            smem,
            smem,
            pl.BlockSpec((X_SIZE, block_rows, rows), lambda i: (0, i, 0)),
            pl.BlockSpec((X_SIZE, block_rows, rows), lambda i: (0, i, 0)),
            whole(X_SIZE, STAT_ROWS, X_SIZE * rows),
            whole(X_SIZE, sent_rows, width),
        ],
        out_specs=[chunk_spec, pl.BlockSpec((chunk, width), lambda i: (i, 0)), whole(1, 128)],
        out_shape=[
            jax.ShapeDtypeStruct((X_SIZE, types, rows), bf16),
            jax.ShapeDtypeStruct((types, width), bf16),
            jax.ShapeDtypeStruct((1, 128), f32),
        ],
        scratch_shapes=[
            pltpu.VMEM((2, X_SIZE * rows), f32),
            pltpu.VMEM((X_SIZE * rows, width), bf16),
            pltpu.VMEM((chunk, X_SIZE * rows), bf16),
        ],
        compiler_params=params(16),
        name="grads",
    )(logit_scale, place, near_exps, far_exps, stats, gathered)
    type_parts = lax.all_to_all(
        type_part.reshape(Z_SIZE, block_rows, width), "gz", 0, 0, tiled=True
    )
    parts = pl.pallas_call(
        mention_kernel,
        grid=(X_SIZE,),
        in_specs=[smem, smem, tile(types, rows)] + table_specs,
        out_specs=[whole(rows, width)] * X_SIZE,
        out_shape=[jax.ShapeDtypeStruct((rows, width), bf16)] * X_SIZE,
        scratch_shapes=[pltpu.VMEM((types, width), bf16)],
        compiler_params=params(16),
        name="mention_part",
    )(logit_scale, place, grads, *table)
    mention_grad = parts[0].astype(f32)
    for s in range(1, X_SIZE):
        mention_grad = mention_grad + paired(
            parts[s], "gx", lambda x, s=s: x ^ s
        ).astype(f32)
    mention_grad = mention_grad.astype(bf16)
    scale_sum = scale_part
    by = 1
    while by < cols:
        scale_sum = scale_sum + paired(scale_sum, "gy", lambda y, by=by: y ^ by)
        by *= 2
    scale_sum = scale_sum + 0.0 * type_parts[0, 0:1, 0:128].astype(f32)
    scale_sums = lax.all_to_all(
        jnp.broadcast_to(scale_sum[None], (Z_SIZE, 1, 128)), "gz", 0, 0, tiled=True
    )
    scale_grad = (jnp.sum(scale_sums[:, 0, 0]) / (rows * devices)).reshape(1)
    type_grad = jnp.sum(type_parts, axis=0, dtype=f32)
    new_table, new_first, new_second = adam_rows(type_table, adam_m, adam_v, type_grad)
    return (new_table, new_first, new_second, mention_grad, scale_grad)


def solution(mesh):
    gx, gy = mesh.devices.shape
    split = Mesh(mesh.devices.reshape(gx // X_SIZE, X_SIZE, gy), ("gz", "gx", "gy"))
    axes = ("gz", "gx", "gy")
    rows = P(axes, None)
    return jax.shard_map(
        per_device,
        mesh=split,
        in_specs=(rows, rows, rows, rows, P(), rows, P(axes), P(axes), P(axes)),
        out_specs=(rows, rows, rows, rows, P()),
        check_vma=False,
    )
```

```python
import jax
import jax.numpy as jnp
from jax import lax
from jax.experimental import pallas as pl
from jax.experimental.pallas import tpu as pltpu
from jax.sharding import Mesh, PartitionSpec as P

beta_one = 0.9
beta_two = 0.999
learn_rate = 0.02
adam_eps = 1e-08
first_fix = 0.9999734386011124
second_fix = 0.09520785288629038

X_SIZE = 4
Z_SIZE = 8
BLOCK = 128
LOW = -1e30
META_ROWS = 32
SLOTS = 16
STAT_ROWS = 8
FIRST_ROWS = 96
SCALE_ROWS = 16
f32 = jnp.float32
bf16 = jnp.bfloat16


def cast_kernel(t_ref, out_ref):
    block = t_ref[...].astype(bf16)
    for k in range(out_ref.shape[0]):
        out_ref[k] = block


def pack_kernel(
    cols, list_hbm, len_hbm, slot_hbm, row_hbm, m_hbm, out_ref, list_ref, len_ref, slot_ref, row_ref, sems
):
    rows, width = m_hbm.shape
    pairs = [(list_hbm, list_ref), (len_hbm, len_ref), (slot_hbm, slot_ref), (row_hbm, row_ref)]
    pairs.append((m_hbm, out_ref.at[pl.ds(0, rows), :]))
    copies = [pltpu.make_async_copy(src, dst, sems.at[i]) for i, (src, dst) in enumerate(pairs)]
    for copy in copies:
        copy.start()
    for copy in copies[:4]:
        copy.wait()
    owners = lax.div(list_ref[...], cols).astype(f32)
    lens = len_ref[...]
    first = lax.broadcasted_iota(jnp.int32, (1, rows), 1) < BLOCK
    length = jnp.where(first, lens[:, 0:1], lens[:, 1:2])
    slot = slot_ref[...]
    gold = jnp.zeros((1, rows), f32)
    lines = []
    for k in range(SLOTS):
        owner = jnp.where(first, owners[0:1, k : k + 1], owners[1:2, k : k + 1])
        gold = gold + jnp.where(slot == k, owner, 0.0)
        lines.append(jnp.where(length > k, owner, -1.0))
    lines += [gold, row_ref[...].astype(f32)]
    lines.append(jnp.zeros((META_ROWS - len(lines), rows), f32))
    out_ref[rows : rows + META_ROWS, :] = jnp.zeros((META_ROWS, width), bf16)
    out_ref[rows : rows + META_ROWS, 0:rows] = jnp.concatenate(lines, axis=0).astype(bf16)
    copies[4].wait()


def owner_at(place_ref, line):
    return (line * X_SIZE + place_ref[1]).astype(f32)


def tile_from(place_ref, step):
    return jnp.bitwise_xor(place_ref[1], step)


def join_types(place_ref, near_ref, low_ref, high_ref, tile_ref):
    parity = lax.rem(place_ref[0], 2)
    half = Z_SIZE // 4
    for k in range(Z_SIZE // 2):
        other = low_ref[k] if k < half else high_ref[k - half]
        tile_ref[pl.ds(pl.multiple_of((2 * k + parity) * BLOCK, BLOCK), BLOCK), :] = near_ref[k]
        tile_ref[pl.ds(pl.multiple_of((2 * k + 1 - parity) * BLOCK, BLOCK), BLOCK), :] = other


def score_half(factor, place_ref, shift, m_ref, tile_ref, raw_ref, exp_ref):
    rows = m_ref.shape[1] - META_ROWS
    raw_ref[...] = lax.dot_general(
        tile_ref[...], m_ref[0, 0:rows, :], (((1,), (1,)), ((), ())), preferred_element_type=f32
    )
    meta = m_ref[0, rows : rows + META_ROWS, 0:rows].astype(f32)
    owners = meta[0:SLOTS, :]
    gold_owner = meta[SLOTS : SLOTS + 1, :]
    gold_row = meta[SLOTS + 1 : SLOTS + 2, :].astype(jnp.int32)
    ids = lax.broadcasted_iota(jnp.int32, (BLOCK, rows), 0)
    top = jnp.full((1, rows), LOW, f32)
    gold_raw = jnp.zeros((1, rows), f32)
    lives = []
    for k in range(Z_SIZE // 2):
        owner = owner_at(place_ref, 2 * k + shift)
        lives.append(jnp.max(jnp.where(owners == owner, 1.0, 0.0), axis=0, keepdims=True) > 0.0)
        raw = raw_ref[k * BLOCK : (k + 1) * BLOCK, :]
        top = jnp.maximum(top, jnp.where(lives[k], jnp.max(raw, axis=0, keepdims=True), LOW))
        gold = jnp.where(gold_owner == owner, gold_row, -1)
        gold_raw = gold_raw + jnp.sum(jnp.where(ids == gold, raw, 0.0), axis=0, keepdims=True)
    total = jnp.zeros((1, rows), f32)
    mass = jnp.zeros((1, rows), f32)
    for k in range(Z_SIZE // 2):
        below = jnp.where(lives[k], top, -LOW)
        gap = raw_ref[k * BLOCK : (k + 1) * BLOCK, :] - below
        weights = jnp.exp(factor * gap)
        exp_ref[0, k * BLOCK : (k + 1) * BLOCK, :] = weights
        total = total + jnp.sum(weights, axis=0, keepdims=True)
        mass = mass + jnp.sum(weights * gap, axis=0, keepdims=True)
    return top, total, mass, gold_raw


def near_kernel(factor_ref, place_ref, m_ref, near_ref, exp_ref, stat_ref, tile_ref, raw_ref):
    step = pl.program_id(0)

    @pl.when(step == 0)
    def _():
        for k in range(near_ref.shape[0]):
            tile_ref[k * BLOCK : (k + 1) * BLOCK, :] = near_ref[k]

    shift = lax.rem(place_ref[0], 2)
    stats = score_half(factor_ref[0], place_ref, shift, m_ref, tile_ref, raw_ref, exp_ref)
    rows = stats[0].shape[1]
    rest = jnp.zeros((STAT_ROWS - len(stats), rows), f32)
    stat_ref[0] = jnp.concatenate(list(stats) + [rest], axis=0)


def far_kernel(
    factor_ref, place_ref, m_ref, low_ref, high_ref, part_ref, exp_ref, stat_ref, tile_ref, raw_ref
):
    step = pl.program_id(0)

    @pl.when(step == 0)
    def _():
        half = low_ref.shape[0]
        for k in range(2 * half):
            other = low_ref[k] if k < half else high_ref[k - half]
            tile_ref[k * BLOCK : (k + 1) * BLOCK, :] = other

    shift = 1 - lax.rem(place_ref[0], 2)
    top, total, mass, gold_raw = score_half(
        factor_ref[0], place_ref, shift, m_ref, tile_ref, raw_ref, exp_ref
    )
    rows = top.shape[1]
    near = part_ref[0]
    lines = [near[0:3, :], top, total, mass, gold_raw + near[3:4, :]]
    lines.append(jnp.zeros((STAT_ROWS - 7, rows), f32))
    stat = jnp.concatenate(lines, axis=0)
    at = pl.multiple_of(tile_from(place_ref, step) * rows, BLOCK)
    for d in range(stat_ref.shape[0]):
        stat_ref[d, :, pl.ds(at, rows)] = stat


def merge_stats(factor, place_ref, stat_ref, share_ref, scale_ref):
    tops, sums, masses = [
        jnp.concatenate([stat_ref[:, r, :], stat_ref[:, r + 3, :]], axis=0) for r in range(3)
    ]
    top = jnp.max(tops, axis=0, keepdims=True)
    shares = jnp.exp(factor * (tops - top))
    total = jnp.sum(sums * shares, axis=0, keepdims=True)
    masses = masses + sums * tops
    mass = jnp.sum(jnp.where(sums > 0.0, masses * shares, 0.0), axis=0, keepdims=True)
    scale = mass / total - jnp.sum(stat_ref[:, 6, :], axis=0, keepdims=True)
    scale_ref[...] = jnp.broadcast_to(jnp.sum(scale, axis=1, keepdims=True), scale_ref.shape)
    ids = lax.broadcasted_iota(jnp.int32, tops.shape, 0)
    for h in range(2):
        mine = ids == place_ref[1] + h * X_SIZE
        own = jnp.max(jnp.where(mine, tops, LOW), axis=0, keepdims=True)
        share_ref[h : h + 1, :] = jnp.exp(factor * (own - top) - jnp.log(total))


def grads_kernel(
    factor_ref, place_ref, near_ref, far_ref, stat_ref, m_ref, g_ref, first_ref, second_ref, scale_ref, share_ref, rows_ref, grad_ref
):
    step = pl.program_id(0)
    factor = factor_ref[0]
    rows = m_ref.shape[1] - META_ROWS
    chunk = grad_ref.shape[0]

    @pl.when(step == 0)
    def _():
        merge_stats(factor, place_ref, stat_ref, share_ref, scale_ref)
        for s in range(X_SIZE):
            rows_ref[s * rows : (s + 1) * rows, :] = m_ref[s, 0:rows, :]

    ids = lax.broadcasted_iota(jnp.int32, (BLOCK, rows), 0)
    parity = lax.rem(place_ref[0], 2)
    for s in range(X_SIZE):
        at = pl.multiple_of(tile_from(place_ref, s) * rows, BLOCK)
        meta = m_ref[s, rows + SLOTS : rows + META_ROWS, 0:rows].astype(f32)
        gold_owner = meta[0:1, :]
        gold_row = meta[1:2, :]
        for h, exp_ref in enumerate((near_ref, far_ref)):
            place = parity if h == 0 else 1 - parity
            owner = owner_at(place_ref, 2 * step + place)
            gold = jnp.where(gold_owner == owner, gold_row, -1.0).astype(jnp.int32)
            weights = share_ref[h : h + 1, pl.ds(at, rows)] * exp_ref[s]
            grad = (weights - jnp.where(ids == gold, 1.0, 0.0)).astype(bf16)
            line = pl.ds(pl.multiple_of(place * BLOCK, BLOCK), BLOCK)
            g_ref[s, line, :] = grad
            grad_ref[line, s * rows : (s + 1) * rows] = grad
    part = jnp.dot(grad_ref[...], rows_ref[...], preferred_element_type=f32)
    part = (factor * part).astype(bf16)
    for c in range(chunk // BLOCK):
        at = c * BLOCK
        first_ref[c] = part[at : at + FIRST_ROWS, :]
        second_ref[c, 0 : BLOCK - FIRST_ROWS, :] = part[at + FIRST_ROWS : at + BLOCK, :]
        second_ref[c, BLOCK - FIRST_ROWS :, :] = jnp.zeros((SCALE_ROWS, part.shape[1]), bf16)


def mention_kernel(factor_ref, place_ref, scale_ref, g_ref, near_ref, low_ref, high_ref, *refs):
    out_refs, tile_ref = refs[:X_SIZE], refs[-1]
    step = pl.program_id(0)

    @pl.when(step == 0)
    def _():
        join_types(place_ref, near_ref, low_ref, high_ref, tile_ref)

    part = lax.dot_general(
        g_ref[0], tile_ref[...], (((0,), (0,)), ((), ())), preferred_element_type=f32
    )
    part = (factor_ref[0] * part).astype(bf16)
    for s, out_ref in enumerate(out_refs):

        @pl.when(step == s)
        def _(out_ref=out_ref):
            out_ref[...] = part


def adam_rows(type_table, adam_m, adam_v, type_grad):
    moment_one = beta_one * adam_m + (1.0 - beta_one) * type_grad
    moment_two = beta_two * adam_v + (1.0 - beta_two) * type_grad * type_grad
    updated = type_table - learn_rate * (moment_one / first_fix) / (
        jnp.sqrt(moment_two / second_fix) + adam_eps
    )
    return (updated, moment_one, moment_two)


def params(mib=60):
    return pltpu.CompilerParams(vmem_limit_bytes=mib * 1024 * 1024)


def paired(array, axis, partner):
    return lax.ppermute(array, axis, [(i, partner(i)) for i in range(lax.axis_size(axis))])


def per_device(
    mentions,
    type_table,
    adam_m,
    adam_v,
    logit_scale,
    block_lists,
    list_lengths,
    gold_slot,
    gold_row,
):
    cols = lax.axis_size("gy")
    devices = Z_SIZE * X_SIZE * cols
    block_rows, width = type_table.shape
    rows = mentions.shape[0]
    sent_rows = rows + META_ROWS
    types = Z_SIZE * block_rows
    smem = pl.BlockSpec(memory_space=pltpu.SMEM)
    hbm = pl.BlockSpec(memory_space=pltpu.HBM)
    place = jnp.stack([lax.axis_index("gz"), lax.axis_index("gx")]).astype(jnp.int32)
    half = Z_SIZE // 2

    def tile(*shape):
        return pl.BlockSpec((1,) + shape, lambda j: (j, 0, 0))

    def whole(*shape):
        return pl.BlockSpec(shape, lambda j: (0,) * len(shape))

    copies = pl.pallas_call(
        cast_kernel,
        out_shape=jax.ShapeDtypeStruct((half, block_rows, width), bf16),
        compiler_params=params(),
        name="cast",
    )(type_table)
    parities = [list(range(p, Z_SIZE, 2)) for p in range(2)]
    near = lax.all_to_all(copies, "gz", 0, 0, tiled=True, axis_index_groups=parities)
    low = paired(near[: half // 2], "gz", lambda z: z ^ 1)
    high = paired(near[half // 2 :], "gz", lambda z: ((z + 1) ^ 1) - 1 & Z_SIZE - 1)
    table = (near, low, high)
    table_specs = [whole(t.shape[0], block_rows, width) for t in table]
    packed = pl.pallas_call(
        lambda *refs: pack_kernel(cols, *refs),
        in_specs=[hbm] * 5,
        out_shape=jax.ShapeDtypeStruct((sent_rows, width), bf16),
        scratch_shapes=[
            pltpu.VMEM((2, SLOTS), jnp.int32),
            pltpu.VMEM((1, 2), jnp.int32),
            pltpu.VMEM((1, rows), jnp.int32),
            pltpu.VMEM((1, rows), jnp.int32),
            pltpu.SemaphoreType.DMA((5,)),
        ],
        compiler_params=params(),
        name="pack",
    )(
        block_lists,
        list_lengths.reshape(1, 2),
        gold_slot.reshape(1, rows),
        gold_row.reshape(1, rows),
        mentions,
    )
    gathered = jnp.stack(
        [packed] + [paired(packed, "gx", lambda x, s=s: x ^ s) for s in range(1, X_SIZE)]
    )

    half_types = half * block_rows
    scratch = [pltpu.VMEM((half_types, width), bf16), pltpu.VMEM((half_types, rows), f32)]
    exps_shape = jax.ShapeDtypeStruct((X_SIZE, half_types, rows), f32)
    near_exps, near_stats = pl.pallas_call(
        near_kernel,
        grid=(X_SIZE,),
        in_specs=[smem, smem, tile(sent_rows, width)] + table_specs[:1],
        out_specs=[tile(half_types, rows), tile(STAT_ROWS, rows)],
        out_shape=[exps_shape, jax.ShapeDtypeStruct((X_SIZE, STAT_ROWS, rows), f32)],
        scratch_shapes=scratch,
        compiler_params=params(16),
        name="near_scores",
    )(logit_scale, place, gathered, near)
    far_exps, stats = pl.pallas_call(
        far_kernel,
        grid=(X_SIZE,),
        in_specs=[smem, smem, tile(sent_rows, width)] + table_specs[1:] + [tile(STAT_ROWS, rows)],
        out_specs=[tile(half_types, rows), whole(X_SIZE, STAT_ROWS, X_SIZE * rows)],
        out_shape=[exps_shape, jax.ShapeDtypeStruct((X_SIZE, STAT_ROWS, X_SIZE * rows), f32)],
        scratch_shapes=scratch,
        compiler_params=params(16),
        name="far_scores",
    )(logit_scale, place, gathered, low, high, near_stats)
    stats = lax.all_to_all(stats, "gx", 0, 0, tiled=True)
    chunk = 2 * block_rows
    last_rows = block_rows - FIRST_ROWS
    second_rows = last_rows + SCALE_ROWS
    chunk_spec = pl.BlockSpec((X_SIZE, chunk, rows), lambda i: (0, i, 0))
    grads, first_part, second_part, scale_sum = pl.pallas_call(
        grads_kernel,
        grid=(types // chunk,),
        in_specs=[
            smem,
            smem,
            pl.BlockSpec((X_SIZE, block_rows, rows), lambda i: (0, i, 0)),
            pl.BlockSpec((X_SIZE, block_rows, rows), lambda i: (0, i, 0)),
            whole(X_SIZE, STAT_ROWS, X_SIZE * rows),
            whole(X_SIZE, sent_rows, width),
        ],
        out_specs=[
            chunk_spec,
            pl.BlockSpec((2, FIRST_ROWS, width), lambda i: (i, 0, 0)),
            pl.BlockSpec((2, second_rows, width), lambda i: (i, 0, 0)),
            whole(1, 128),
        ],
        out_shape=[
            jax.ShapeDtypeStruct((X_SIZE, types, rows), bf16),
            jax.ShapeDtypeStruct((Z_SIZE, FIRST_ROWS, width), bf16),
            jax.ShapeDtypeStruct((Z_SIZE, second_rows, width), bf16),
            jax.ShapeDtypeStruct((1, 128), f32),
        ],
        scratch_shapes=[
            pltpu.VMEM((2, X_SIZE * rows), f32),
            pltpu.VMEM((X_SIZE * rows, width), bf16),
            pltpu.VMEM((chunk, X_SIZE * rows), bf16),
        ],
        compiler_params=params(16),
        name="grads",
    )(logit_scale, place, near_exps, far_exps, stats, gathered)
    first = lax.all_to_all(first_part, "gz", 0, 0, tiled=True)
    by = 1
    while by < cols:
        scale_sum = scale_sum + paired(scale_sum, "gy", lambda y, by=by: y ^ by)
        by *= 2
    scale_sum = scale_sum + 0.0 * first[0, 0:1, 0:128].astype(f32)
    hi = lax.reduce_precision(scale_sum, 8, 7)
    mid = lax.reduce_precision(scale_sum - hi, 8, 7)
    pieces = jnp.concatenate([hi, mid, scale_sum - hi - mid], axis=1).astype(bf16)
    pieces = jnp.broadcast_to(pieces[None], (Z_SIZE, SCALE_ROWS, pieces.shape[1]))
    second_part = lax.dynamic_update_slice(second_part, pieces, (0, last_rows, 0))
    second = lax.all_to_all(second_part, "gz", 0, 0, tiled=True)
    parts = pl.pallas_call(
        mention_kernel,
        grid=(X_SIZE,),
        in_specs=[smem, smem, whole(1, 128), tile(types, rows)] + table_specs,
        out_specs=[whole(rows, width)] * X_SIZE,
        out_shape=[jax.ShapeDtypeStruct((rows, width), bf16)] * X_SIZE,
        scratch_shapes=[pltpu.VMEM((types, width), bf16)],
        compiler_params=params(16),
        name="mention_part",
    )(logit_scale, place, scale_sum, grads, *table)
    mention_grad = parts[0].astype(f32)
    for s in range(1, X_SIZE):
        mention_grad = mention_grad + paired(
            parts[s], "gx", lambda x, s=s: x ^ s
        ).astype(f32)
    mention_grad = mention_grad.astype(bf16)
    pieces = second[:, last_rows, 0 : 3 * 128 : 128].astype(f32)
    scale_grad = (jnp.sum(pieces) / (rows * devices)).reshape(1)
    type_grad = jnp.concatenate(
        [
            jnp.sum(first, axis=0, dtype=f32),
            jnp.sum(second[:, 0:last_rows], axis=0, dtype=f32),
        ]
    )
    new_table, new_first, new_second = adam_rows(type_table, adam_m, adam_v, type_grad)
    return (new_table, new_first, new_second, mention_grad, scale_grad)


def solution(mesh):
    gx, gy = mesh.devices.shape
    split = Mesh(mesh.devices.reshape(gx // X_SIZE, X_SIZE, gy), ("gz", "gx", "gy"))
    axes = ("gz", "gx", "gy")
    rows = P(axes, None)
    return jax.shard_map(
        per_device,
        mesh=split,
        in_specs=(rows, rows, rows, rows, P(), rows, P(axes), P(axes), P(axes)),
        out_specs=(rows, rows, rows, rows, P()),
        check_vma=False,
    )
```

```python
import jax
import jax.numpy as jnp
from jax import lax
from jax.experimental import pallas as pl
from jax.experimental.pallas import tpu as pltpu
from jax.sharding import Mesh, PartitionSpec as P

beta_one = 0.9
beta_two = 0.999
learn_rate = 0.02
adam_eps = 1e-08
first_fix = 0.9999734386011124
second_fix = 0.09520785288629038

X_SIZE = 4
Z_SIZE = 8
BLOCK = 128
LOW = -1e30
META_ROWS = 32
SLOTS = 16
STAT_ROWS = 8
f32 = jnp.float32
bf16 = jnp.bfloat16


def cast_kernel(t_ref, out_ref):
    block = t_ref[...].astype(bf16)
    for k in range(out_ref.shape[0]):
        out_ref[k] = block


def pack_kernel(
    cols, list_hbm, len_hbm, slot_hbm, row_hbm, m_hbm, out_ref, list_ref, len_ref, slot_ref, row_ref, sems
):
    rows, width = m_hbm.shape
    pairs = [(list_hbm, list_ref), (len_hbm, len_ref), (slot_hbm, slot_ref), (row_hbm, row_ref)]
    pairs.append((m_hbm, out_ref.at[pl.ds(0, rows), :]))
    copies = [pltpu.make_async_copy(src, dst, sems.at[i]) for i, (src, dst) in enumerate(pairs)]
    for copy in copies:
        copy.start()
    for copy in copies[:4]:
        copy.wait()
    owners = lax.div(list_ref[...], cols).astype(f32)
    lens = len_ref[...]
    first = lax.broadcasted_iota(jnp.int32, (1, rows), 1) < BLOCK
    length = jnp.where(first, lens[:, 0:1], lens[:, 1:2])
    slot = slot_ref[...]
    gold = jnp.zeros((1, rows), f32)
    lines = []
    for k in range(SLOTS):
        owner = jnp.where(first, owners[0:1, k : k + 1], owners[1:2, k : k + 1])
        gold = gold + jnp.where(slot == k, owner, 0.0)
        lines.append(jnp.where(length > k, owner, -1.0))
    lines += [gold, row_ref[...].astype(f32)]
    lines.append(jnp.zeros((META_ROWS - len(lines), rows), f32))
    out_ref[rows : rows + META_ROWS, :] = jnp.zeros((META_ROWS, width), bf16)
    out_ref[rows : rows + META_ROWS, 0:rows] = jnp.concatenate(lines, axis=0).astype(bf16)
    copies[4].wait()


def owner_at(place_ref, line):
    return (line * X_SIZE + place_ref[1]).astype(f32)


def tile_from(place_ref, step):
    return jnp.bitwise_xor(place_ref[1], step)


def join_types(place_ref, near_ref, low_ref, high_ref, tile_ref):
    parity = lax.rem(place_ref[0], 2)
    half = Z_SIZE // 4
    for k in range(Z_SIZE // 2):
        other = low_ref[k] if k < half else high_ref[k - half]
        tile_ref[pl.ds(pl.multiple_of((2 * k + parity) * BLOCK, BLOCK), BLOCK), :] = near_ref[k]
        tile_ref[pl.ds(pl.multiple_of((2 * k + 1 - parity) * BLOCK, BLOCK), BLOCK), :] = other


def score_half(factor, place_ref, shift, m_ref, tile_ref, raw_ref, exp_ref):
    rows = m_ref.shape[1] - META_ROWS
    raw_ref[...] = lax.dot_general(
        tile_ref[...], m_ref[0, 0:rows, :], (((1,), (1,)), ((), ())), preferred_element_type=f32
    )
    meta = m_ref[0, rows : rows + META_ROWS, 0:rows].astype(f32)
    owners = meta[0:SLOTS, :]
    gold_owner = meta[SLOTS : SLOTS + 1, :]
    gold_row = meta[SLOTS + 1 : SLOTS + 2, :].astype(jnp.int32)
    ids = lax.broadcasted_iota(jnp.int32, (BLOCK, rows), 0)
    top = jnp.full((1, rows), LOW, f32)
    gold_raw = jnp.zeros((1, rows), f32)
    lives = []
    for k in range(Z_SIZE // 2):
        owner = owner_at(place_ref, 2 * k + shift)
        lives.append(jnp.max(jnp.where(owners == owner, 1.0, 0.0), axis=0, keepdims=True) > 0.0)
        raw = raw_ref[k * BLOCK : (k + 1) * BLOCK, :]
        top = jnp.maximum(top, jnp.where(lives[k], jnp.max(raw, axis=0, keepdims=True), LOW))
        gold = jnp.where(gold_owner == owner, gold_row, -1)
        gold_raw = gold_raw + jnp.sum(jnp.where(ids == gold, raw, 0.0), axis=0, keepdims=True)
    total = jnp.zeros((1, rows), f32)
    mass = jnp.zeros((1, rows), f32)
    for k in range(Z_SIZE // 2):
        below = jnp.where(lives[k], top, -LOW)
        gap = raw_ref[k * BLOCK : (k + 1) * BLOCK, :] - below
        weights = jnp.exp(factor * gap)
        exp_ref[0, k * BLOCK : (k + 1) * BLOCK, :] = weights
        total = total + jnp.sum(weights, axis=0, keepdims=True)
        mass = mass + jnp.sum(weights * gap, axis=0, keepdims=True)
    return top, total, mass, gold_raw


def near_kernel(factor_ref, place_ref, m_ref, near_ref, exp_ref, stat_ref, tile_ref, raw_ref):
    step = pl.program_id(0)

    @pl.when(step == 0)
    def _():
        for k in range(near_ref.shape[0]):
            tile_ref[k * BLOCK : (k + 1) * BLOCK, :] = near_ref[k]

    shift = lax.rem(place_ref[0], 2)
    stats = score_half(factor_ref[0], place_ref, shift, m_ref, tile_ref, raw_ref, exp_ref)
    rows = stats[0].shape[1]
    rest = jnp.zeros((STAT_ROWS - len(stats), rows), f32)
    stat_ref[0] = jnp.concatenate(list(stats) + [rest], axis=0)


def far_kernel(
    factor_ref, place_ref, m_ref, low_ref, high_ref, part_ref, exp_ref, stat_ref, tile_ref, raw_ref
):
    step = pl.program_id(0)

    @pl.when(step == 0)
    def _():
        half = low_ref.shape[0]
        for k in range(2 * half):
            other = low_ref[k] if k < half else high_ref[k - half]
            tile_ref[k * BLOCK : (k + 1) * BLOCK, :] = other

    shift = 1 - lax.rem(place_ref[0], 2)
    top, total, mass, gold_raw = score_half(
        factor_ref[0], place_ref, shift, m_ref, tile_ref, raw_ref, exp_ref
    )
    rows = top.shape[1]
    near = part_ref[0]
    lines = [near[0:3, :], top, total, mass, gold_raw + near[3:4, :]]
    lines.append(jnp.zeros((STAT_ROWS - 7, rows), f32))
    stat = jnp.concatenate(lines, axis=0)
    at = pl.multiple_of(tile_from(place_ref, step) * rows, BLOCK)
    for d in range(stat_ref.shape[0]):
        stat_ref[d, :, pl.ds(at, rows)] = stat


def merge_stats(factor, place_ref, stat_ref, share_ref, scale_ref):
    tops, sums, masses = [
        jnp.concatenate([stat_ref[:, r, :], stat_ref[:, r + 3, :]], axis=0) for r in range(3)
    ]
    top = jnp.max(tops, axis=0, keepdims=True)
    shares = jnp.exp(factor * (tops - top))
    total = jnp.sum(sums * shares, axis=0, keepdims=True)
    masses = masses + sums * tops
    mass = jnp.sum(jnp.where(sums > 0.0, masses * shares, 0.0), axis=0, keepdims=True)
    scale = mass / total - jnp.sum(stat_ref[:, 6, :], axis=0, keepdims=True)
    scale = jnp.sum(scale, axis=1, keepdims=True)
    scale_ref[...] = jnp.broadcast_to(scale[None], scale_ref.shape)
    ids = lax.broadcasted_iota(jnp.int32, tops.shape, 0)
    for h in range(2):
        mine = ids == place_ref[1] + h * X_SIZE
        own = jnp.max(jnp.where(mine, tops, LOW), axis=0, keepdims=True)
        share_ref[h : h + 1, :] = jnp.exp(factor * (own - top) - jnp.log(total))


def grads_kernel(
    factor_ref, place_ref, near_ref, far_ref, stat_ref, m_ref, g_ref, own_ref, low_ref, high_ref, scale_ref, share_ref, rows_ref, grad_ref
):
    step = pl.program_id(0)
    factor = factor_ref[0]
    rows = m_ref.shape[1] - META_ROWS

    @pl.when(step == 0)
    def _():
        merge_stats(factor, place_ref, stat_ref, share_ref, scale_ref)
        for s in range(X_SIZE):
            rows_ref[s * rows : (s + 1) * rows, :] = m_ref[s, 0:rows, :]

    ids = lax.broadcasted_iota(jnp.int32, (BLOCK, rows), 0)
    parity = lax.rem(place_ref[0], 2)
    for s in range(X_SIZE):
        at = pl.multiple_of(tile_from(place_ref, s) * rows, BLOCK)
        meta = m_ref[s, rows + SLOTS : rows + META_ROWS, 0:rows].astype(f32)
        gold_owner = meta[0:1, :]
        gold_row = meta[1:2, :]
        for h, exp_ref in enumerate((near_ref, far_ref)):
            place = parity if h == 0 else 1 - parity
            owner = owner_at(place_ref, 2 * step + place)
            gold = jnp.where(gold_owner == owner, gold_row, -1.0).astype(jnp.int32)
            weights = share_ref[h : h + 1, pl.ds(at, rows)] * exp_ref[s]
            grad = (weights - jnp.where(ids == gold, 1.0, 0.0)).astype(bf16)
            line = pl.ds(pl.multiple_of(place * BLOCK, BLOCK), BLOCK)
            g_ref[s, line, :] = grad
            grad_ref[h * BLOCK : (h + 1) * BLOCK, s * rows : (s + 1) * rows] = grad
    part = jnp.dot(grad_ref[...], rows_ref[...], preferred_element_type=f32)
    part = (factor * part).astype(bf16)
    own_ref[0] = part[0:BLOCK, :]
    half = low_ref.shape[0]
    for k in range(2 * half):

        @pl.when(step == k)
        def _(k=k):
            out_ref = low_ref if k < half else high_ref
            out_ref[k % half] = part[BLOCK:, :]


def mention_kernel(factor_ref, place_ref, scale_ref, g_ref, near_ref, low_ref, high_ref, *refs):
    out_refs, tile_ref = refs[:X_SIZE], refs[-1]
    step = pl.program_id(0)

    @pl.when(step == 0)
    def _():
        join_types(place_ref, near_ref, low_ref, high_ref, tile_ref)

    part = lax.dot_general(
        g_ref[0], tile_ref[...], (((0,), (0,)), ((), ())), preferred_element_type=f32
    )
    part = (factor_ref[0] * part).astype(bf16)
    for s, out_ref in enumerate(out_refs):

        @pl.when(step == s)
        def _(out_ref=out_ref):
            out_ref[...] = part


def adam_rows(type_table, adam_m, adam_v, type_grad):
    moment_one = beta_one * adam_m + (1.0 - beta_one) * type_grad
    moment_two = beta_two * adam_v + (1.0 - beta_two) * type_grad * type_grad
    updated = type_table - learn_rate * (moment_one / first_fix) / (
        jnp.sqrt(moment_two / second_fix) + adam_eps
    )
    return (updated, moment_one, moment_two)


def params(mib=60):
    return pltpu.CompilerParams(vmem_limit_bytes=mib * 1024 * 1024)


def paired(array, axis, partner):
    return lax.ppermute(array, axis, [(i, partner(i)) for i in range(lax.axis_size(axis))])


def per_device(
    mentions,
    type_table,
    adam_m,
    adam_v,
    logit_scale,
    block_lists,
    list_lengths,
    gold_slot,
    gold_row,
):
    cols = lax.axis_size("gy")
    devices = Z_SIZE * X_SIZE * cols
    block_rows, width = type_table.shape
    rows = mentions.shape[0]
    sent_rows = rows + META_ROWS
    types = Z_SIZE * block_rows
    smem = pl.BlockSpec(memory_space=pltpu.SMEM)
    hbm = pl.BlockSpec(memory_space=pltpu.HBM)
    place = jnp.stack([lax.axis_index("gz"), lax.axis_index("gx")]).astype(jnp.int32)
    half = Z_SIZE // 2

    def tile(*shape):
        return pl.BlockSpec((1,) + shape, lambda j: (j, 0, 0))

    def whole(*shape):
        return pl.BlockSpec(shape, lambda j: (0,) * len(shape))

    copies = pl.pallas_call(
        cast_kernel,
        out_shape=jax.ShapeDtypeStruct((half, block_rows, width), bf16),
        compiler_params=params(),
        name="cast",
    )(type_table)
    parities = [list(range(p, Z_SIZE, 2)) for p in range(2)]
    near = lax.all_to_all(copies, "gz", 0, 0, tiled=True, axis_index_groups=parities)
    low = paired(near[: half // 2], "gz", lambda z: z ^ 1)
    high = paired(near[half // 2 :], "gz", lambda z: ((z + 1) ^ 1) - 1 & Z_SIZE - 1)
    table = (near, low, high)
    table_specs = [whole(t.shape[0], block_rows, width) for t in table]
    packed = pl.pallas_call(
        lambda *refs: pack_kernel(cols, *refs),
        in_specs=[hbm] * 5,
        out_shape=jax.ShapeDtypeStruct((sent_rows, width), bf16),
        scratch_shapes=[
            pltpu.VMEM((2, SLOTS), jnp.int32),
            pltpu.VMEM((1, 2), jnp.int32),
            pltpu.VMEM((1, rows), jnp.int32),
            pltpu.VMEM((1, rows), jnp.int32),
            pltpu.SemaphoreType.DMA((5,)),
        ],
        compiler_params=params(),
        name="pack",
    )(
        block_lists,
        list_lengths.reshape(1, 2),
        gold_slot.reshape(1, rows),
        gold_row.reshape(1, rows),
        mentions,
    )
    gathered = jnp.stack(
        [packed] + [paired(packed, "gx", lambda x, s=s: x ^ s) for s in range(1, X_SIZE)]
    )

    half_types = half * block_rows
    scratch = [pltpu.VMEM((half_types, width), bf16), pltpu.VMEM((half_types, rows), f32)]
    exps_shape = jax.ShapeDtypeStruct((X_SIZE, half_types, rows), f32)
    near_exps, near_stats = pl.pallas_call(
        near_kernel,
        grid=(X_SIZE,),
        in_specs=[smem, smem, tile(sent_rows, width)] + table_specs[:1],
        out_specs=[tile(half_types, rows), tile(STAT_ROWS, rows)],
        out_shape=[exps_shape, jax.ShapeDtypeStruct((X_SIZE, STAT_ROWS, rows), f32)],
        scratch_shapes=scratch,
        compiler_params=params(16),
        name="near_scores",
    )(logit_scale, place, gathered, near)
    far_exps, stats = pl.pallas_call(
        far_kernel,
        grid=(X_SIZE,),
        in_specs=[smem, smem, tile(sent_rows, width)] + table_specs[1:] + [tile(STAT_ROWS, rows)],
        out_specs=[tile(half_types, rows), whole(X_SIZE, STAT_ROWS, X_SIZE * rows)],
        out_shape=[exps_shape, jax.ShapeDtypeStruct((X_SIZE, STAT_ROWS, X_SIZE * rows), f32)],
        scratch_shapes=scratch,
        compiler_params=params(16),
        name="far_scores",
    )(logit_scale, place, gathered, low, high, near_stats)
    stats = lax.all_to_all(stats, "gx", 0, 0, tiled=True)
    chunk = 2 * block_rows
    chunk_spec = pl.BlockSpec((X_SIZE, chunk, rows), lambda i: (0, i, 0))
    grads, own_part, low_part, high_part, scale_parts = pl.pallas_call(
        grads_kernel,
        grid=(types // chunk,),
        in_specs=[
            smem,
            smem,
            pl.BlockSpec((X_SIZE, block_rows, rows), lambda i: (0, i, 0)),
            pl.BlockSpec((X_SIZE, block_rows, rows), lambda i: (0, i, 0)),
            whole(X_SIZE, STAT_ROWS, X_SIZE * rows),
            whole(X_SIZE, sent_rows, width),
        ],
        out_specs=[
            chunk_spec,
            tile(block_rows, width),
            whole(half // 2, block_rows, width),
            whole(half // 2, block_rows, width),
            whole(Z_SIZE * cols, 1, 128),
        ],
        out_shape=[
            jax.ShapeDtypeStruct((X_SIZE, types, rows), bf16),
            jax.ShapeDtypeStruct((half, block_rows, width), bf16),
            jax.ShapeDtypeStruct((half // 2, block_rows, width), bf16),
            jax.ShapeDtypeStruct((half // 2, block_rows, width), bf16),
            jax.ShapeDtypeStruct((Z_SIZE * cols, 1, 128), f32),
        ],
        scratch_shapes=[
            pltpu.VMEM((2, X_SIZE * rows), f32),
            pltpu.VMEM((X_SIZE * rows, width), bf16),
            pltpu.VMEM((chunk, X_SIZE * rows), bf16),
        ],
        compiler_params=params(16),
        name="grads",
    )(logit_scale, place, near_exps, far_exps, stats, gathered)
    from_low = paired(low_part, "gz", lambda z: z ^ 1)
    from_high = paired(high_part, "gz", lambda z: ((z + 1) ^ 1) - 1 & Z_SIZE - 1)
    scale_parts = lax.all_to_all(scale_parts, ("gz", "gy"), 0, 0, tiled=True)
    scale_sum = jnp.sum(scale_parts[:, 0, 0])
    scale_grad = (scale_sum / (rows * devices)).reshape(1)
    received = jnp.concatenate([from_low, from_high]).astype(f32)
    own_part = (own_part.astype(f32) + received + 0.0 * scale_sum).astype(bf16)
    type_parts = lax.all_to_all(own_part, "gz", 0, 0, tiled=True, axis_index_groups=parities)
    parts = pl.pallas_call(
        mention_kernel,
        grid=(X_SIZE,),
        in_specs=[smem, smem, smem, tile(types, rows)] + table_specs,
        out_specs=[whole(rows, width)] * X_SIZE,
        out_shape=[jax.ShapeDtypeStruct((rows, width), bf16)] * X_SIZE,
        scratch_shapes=[pltpu.VMEM((types, width), bf16)],
        compiler_params=params(16),
        name="mention_part",
    )(logit_scale, place, scale_grad, grads, *table)
    mention_grad = parts[0].astype(f32)
    for s in range(1, X_SIZE):
        mention_grad = mention_grad + paired(
            parts[s], "gx", lambda x, s=s: x ^ s
        ).astype(f32)
    mention_grad = mention_grad.astype(bf16)
    type_grad = jnp.sum(type_parts, axis=0, dtype=f32)
    new_table, new_first, new_second = adam_rows(type_table, adam_m, adam_v, type_grad)
    return (new_table, new_first, new_second, mention_grad, scale_grad)


def solution(mesh):
    gx, gy = mesh.devices.shape
    split = Mesh(mesh.devices.reshape(gx // X_SIZE, X_SIZE, gy), ("gz", "gx", "gy"))
    axes = ("gz", "gx", "gy")
    rows = P(axes, None)
    return jax.shard_map(
        per_device,
        mesh=split,
        in_specs=(rows, rows, rows, rows, P(), rows, P(axes), P(axes), P(axes)),
        out_specs=(rows, rows, rows, rows, P()),
        check_vma=False,
    )
```
